512 devices in a mesh: site: 16 (over y, core), sector: 32 (over z, x).
Axes of the slice: x: 4, y: 8, z: 8, core: 2. Of those that a mesh axis runs over, the one named last changes fastest.
Arguments:
- mps: bfloat16 [64, 64, 64, 256], P('sector', 'site'), may hold values from -0.75 to 0.75
- left_env: bfloat16 [32, 64, 64, 1088], P('sector', 'site'), may hold values from -6 to 6
- right_env: bfloat16 [32, 64, 64, 1088], P('sector', 'site'), may hold values from -6 to 6
- row_fill: int32 [64, 64], P('sector', 'site'), may hold values from 32 to 64
- col_fill: int32 [64, 64, 4], P('sector', 'site'), may hold values from 32 to 64
- mpo_values: bfloat16 [17, 17, 4], replicated, may hold values from -1.5 to 1.5
- mpo_pattern: int32 [17, 17, 4], replicated, may hold values 0 or 1
Outputs:
- lanczos_vector: float32 [64, 64, 64, 256], P('sector', 'site')
The draws below stay inside these ranges and needn't reach their ends.
All inputs are finite; a program needn't handle non-finite values.
Results may differ from the reference program's by a relative error of at most 0.0094.
Values may be sent and summed in bfloat16 or wider, within the bound.
No kernel may reach another device: no remote copies, remote signals or barrier semaphores. Data moves between devices by JAX's collectives and lax.ppermute only.
A program may use at most 128 MiB of HBM per device.

```python
import jax
import jax.numpy as jnp
from jax import lax

BLK = 64
SEC_DEV = 4
PHYS = 4
WB = 17
SEG = 2
NSEC = 64
SEGMENTS = 32
SITES = 64


def plant(entries, stream_key, smallest, high):
    dims = entries.shape
    index_at = [jax.random.randint(jax.random.fold_in(stream_key, axis), (), 0, dims[axis]) for axis in range(len(dims))]
    entries = entries.at[tuple(index_at)].set(smallest)
    longest = dims.index(max(dims))
    index_at[longest] = (index_at[longest] + 1) % dims[longest]
    return entries.at[tuple(index_at)].set(high)


def shard_levels(own_key, dims, split, least, high):
    gain, own = 1.0, jax.random.fold_in(own_key, 6)
    for dim, shards_of in split:
        heights = jnp.exp(jax.random.uniform(jax.random.fold_in(own, dim), (shards_of,), jnp.float32, least / len(split), high / len(split)))
        gain = gain * jnp.repeat(heights, dims[dim] // shards_of).reshape([-1 if axis == dim else 1 for axis in range(len(dims))])
    return gain


def noise(own_key, dims, scale, most, split=(), held_as=jnp.bfloat16):
    entries = scale * jax.random.normal(own_key, dims, jnp.float32)
    if split:
        entries = entries * shard_levels(own_key, dims, split, -0.22, 0.18)
    return jnp.clip(entries, -most, most).astype(held_as)


def setup_inputs(seed: int = 0) -> dict:
    streams_of = jax.random.split(jax.random.key(seed), 8)
    return {
        "mps": noise(streams_of[0], (SITES, NSEC, BLK, PHYS * BLK), BLK ** -0.5, 0.75, ((0, 32), (1, 16))),
        "left_env": noise(streams_of[1], (SEGMENTS, NSEC, BLK, WB * BLK), 1.0, 6.0, ((0, 32), (1, 16))),
        "right_env": noise(streams_of[2], (SEGMENTS, NSEC, BLK, WB * BLK), 1.0, 6.0, ((0, 32), (1, 16))),
        "row_fill": plant(jax.random.randint(streams_of[3], (SITES, NSEC), BLK // 2, BLK + 1), jax.random.fold_in(streams_of[3], 1), BLK // 2, BLK).astype(jnp.int32),
        "col_fill": plant(jax.random.randint(streams_of[4], (SITES, NSEC, PHYS), BLK // 2, BLK + 1), jax.random.fold_in(streams_of[4], 1), BLK // 2, BLK).astype(jnp.int32),
        "mpo_values": noise(streams_of[5], (WB, WB, PHYS), WB ** -0.5, 1.5),
        "mpo_pattern": plant((jax.random.randint(streams_of[6], (WB, WB, PHYS), 0, 2) < 1).astype(jnp.int32), jax.random.fold_in(streams_of[6], 1), 0, 1),
    }


def stored(value):
    return lax.optimization_barrier(value.astype(jnp.bfloat16)).astype(jnp.float32)

def effective(mps, row_fill, col_fill):
    count, sectors, height, width = mps.shape
    position = jnp.arange(height, dtype=jnp.int32)
    row_keep = position[None, None, :] < row_fill[:, :, None]
    col_keep = (position[None, None, None, :] < col_fill[:, :, :, None]).reshape(count, sectors, width)
    keep = jnp.logical_and(row_keep[:, :, :, None], col_keep[:, :, None, :])
    return mps * keep.astype(mps.dtype)

def sector_roll(value, step_high, step_low):
    grid_view = value.reshape((NSEC // SEC_DEV, SEC_DEV) + value.shape[1:])
    grid_view = jnp.roll(grid_view, (step_high, step_low), axis=(0, 1))
    return grid_view.reshape(value.shape)

def state_cols(value, local_state):
    return value[..., local_state * BLK:(local_state + 1) * BLK]

def left_mixed(environ, site_tensor, wide):
    grid = environ.reshape(environ.shape[0], BLK, WB, BLK).astype(jnp.float32)
    inner_part = stored(jnp.einsum('siwk,skq->swiq', grid, site_tensor.astype(jnp.float32)))
    return stored(jnp.einsum('swiq,wvq->sviq', inner_part, wide.astype(jnp.float32)))

def left_update(environ, site_tensor, wide):
    mixed = left_mixed(environ, site_tensor, wide)
    summed = jnp.zeros(environ.shape, jnp.float32)
    for local_state in range(PHYS):
        site_block = state_cols(site_tensor, local_state).astype(jnp.float32)
        contribution = jnp.einsum('sim,svil->smvl', site_block, state_cols(mixed, local_state))
        contribution = contribution.reshape(environ.shape)
        summed = summed + sector_roll(contribution, local_state // 2, local_state % 2)
    return (summed.astype(jnp.bfloat16), mixed)

def right_update(environ, site_tensor, weights):
    summed = jnp.zeros(environ.shape, jnp.float32)
    for local_state in range(PHYS):
        target = sector_roll(environ, -(local_state // 2), -(local_state % 2)).astype(jnp.float32)
        site_block = state_cols(site_tensor, local_state).astype(jnp.float32)
        inner_part = stored(jnp.einsum('smi,siq->smq', site_block, target))
        inner_part = inner_part.reshape(environ.shape[0], BLK, WB, BLK)
        mixed_part = stored(jnp.einsum('smvk,wv->swmk', inner_part, weights[:, :, local_state].astype(jnp.float32)))
        closed = jnp.einsum('swmk,snk->smwn', mixed_part, site_block)
        summed = summed + closed.reshape(environ.shape)
    return summed.astype(jnp.bfloat16)

def apply_site(mixed, right_side):
    pieces = []
    for local_state in range(PHYS):
        target = sector_roll(right_side, -(local_state // 2), -(local_state % 2)).astype(jnp.float32)
        target = target.reshape(right_side.shape[0], BLK, WB, BLK)
        pieces.append(jnp.einsum('svil,sjvl->sij', state_cols(mixed, local_state), target))
    whole = jnp.concatenate(pieces, axis=2)
    return whole * lax.rsqrt(jnp.mean(whole * whole) + 1e-06)

def reference(mps, left_env, right_env, row_fill, col_fill, mpo_values, mpo_pattern):
    weights = mpo_values * mpo_pattern.astype(jnp.bfloat16)
    wide = jnp.repeat(weights, BLK, axis=2)
    masked = effective(mps, row_fill, col_fill).reshape(SEGMENTS, SEG, NSEC, BLK, PHYS * BLK)

    def sweep(pieces):
        sites, boundary_left, boundary_right = pieces
        left_one, first_mixed = left_update(boundary_left, sites[0], wide)
        left_out, second_mixed = left_update(left_one, sites[1], wide)
        right_one = right_update(boundary_right, sites[1], weights)
        right_out = right_update(right_one, sites[0], weights)
        return (left_one, left_out, right_one, right_out, second_mixed)
    left_one, left_out, right_one, right_out, second_mixed = lax.map(sweep, (masked, left_env, right_env))
    left_in = jnp.concatenate([left_env[:1], left_out[:-1]], axis=0)
    right_in = jnp.concatenate([right_out[1:], right_env[-1:]], axis=0)

    def finish(pieces):
        sites, fresh_left, kept_mixed, inner_right, fresh_right = pieces
        first_result = apply_site(left_mixed(fresh_left, sites[0], wide), inner_right)
        second_result = apply_site(kept_mixed, fresh_right)
        return jnp.stack([first_result, second_result])
    result = lax.map(finish, (masked, left_in, second_mixed, right_one, right_in))
    return result.reshape(SITES, NSEC, BLK, PHYS * BLK)
```

```python
import functools

import jax
import jax.numpy as jnp
from jax import lax
from jax.experimental import pallas as pl
from jax.experimental.pallas import tpu as pltpu
from jax.sharding import PartitionSpec as P

BLK = 64
PHYS = 4
WB = 17
HALF = WB * 128
FULL = 2 * HALF
GROUPS = 8
DEPTH = 144
BF = jnp.bfloat16
F32 = jnp.float32
VMEM_BYTES = 48 * 1024 * 1024


def shape(dims, dtype=BF):
    return jax.ShapeDtypeStruct(dims, dtype)


def call(body, outs, scratch=(), smem=0, operands=(), flops=0):
    in_specs = [
        pl.BlockSpec(memory_space=pltpu.SMEM if i < smem else pltpu.VMEM)
        for i in range(len(operands))
    ]
    single = not isinstance(outs, (list, tuple))
    moved = sum(o.size * o.dtype.itemsize for o in operands)
    out_spec = pl.BlockSpec(memory_space=pltpu.VMEM)
    return pl.pallas_call(
        body,
        out_shape=outs,
        in_specs=in_specs,
        out_specs=out_spec if single else [out_spec] * len(outs),
        scratch_shapes=list(scratch),
        compiler_params=pltpu.CompilerParams(vmem_limit_bytes=VMEM_BYTES),
        cost_estimate=pl.CostEstimate(flops=flops, bytes_accessed=moved, transcendentals=0),
    )(*operands)


def iota(dims, axis):
    return lax.broadcasted_iota(jnp.int32, dims, axis)


def dot(a, b):
    return lax.dot_general(a, b, (((1,), (0,)), ((), ())), preferred_element_type=F32)


def dot_t(a, b):
    return lax.dot_general(a, b, (((1,), (1,)), ((), ())), preferred_element_type=F32)


def target(s, p):
    return (s + p % 2) % 4


def mask_body(rows_ref, cols_ref, mps_ref, all_ref, high_ref):
    row = iota((BLK, 256), 0)
    col = iota((BLK, 256), 1)
    inside = col & (BLK - 1)
    for j in range(2):
        for s in range(4):
            least = jnp.where(col < 64, cols_ref[j, s, 0], cols_ref[j, s, 1])
            most = jnp.where(col < 192, cols_ref[j, s, 2], cols_ref[j, s, 3])
            limit = jnp.where(col < 128, least, most)
            keep = jnp.logical_and(row < rows_ref[j, s], inside < limit)
            kept = jnp.where(keep, mps_ref[j, s].astype(F32), 0.0).astype(BF)
            all_ref[j, s * BLK : (s + 1) * BLK, :] = kept
            high_ref[j, s * BLK : (s + 1) * BLK, :] = kept[:, 128:]


def spread(block, step):
    tiled = jnp.concatenate([block] * 4, axis=1)
    goal = ((iota((256, 256), 0) >> 6) + step) & 3
    return jnp.where(goal == (iota((256, 256), 1) >> 6), tiled, 0.0).astype(BF)


def flipped(values, states):
    turned = values.T
    rows = []
    for t in range(4):
        parts = []
        for p in range(states):
            s = (t - p % 2) % 4
            parts.append(turned[p * BLK : (p + 1) * BLK, s * BLK : (s + 1) * BLK])
        rows.append(jnp.concatenate(parts, axis=1))
    return jnp.concatenate(rows, axis=0).astype(BF)


def enlarge(small, out_ref):
    rows = 4 * WB * 8
    up = jnp.where((iota((rows, 4 * WB), 0) >> 3) == iota((rows, 4 * WB), 1), 1.0, 0.0)
    out = jnp.where((iota((WB, DEPTH), 1) >> 3) == iota((WB, DEPTH), 0), 1.0, 0.0)
    tall = dot(up.astype(BF), small).astype(BF)
    wide = dot(tall, out.astype(BF))
    same = (iota((rows, DEPTH), 0) & 7) == (iota((rows, DEPTH), 1) & 7)
    out_ref[...] = jnp.where(same, wide, 0.0).astype(BF)


def own_ops_body(a_ref, wl_ref, wr_ref, b_ref, at_ref, kl_ref, kr_ref):
    for j in range(2):
        values = a_ref[j].astype(F32)
        for p in range(PHYS):
            b_ref[j, p] = spread(values[:, p * BLK : (p + 1) * BLK], p % 2)
        at_ref[j] = flipped(values[:, :128], 2)
    enlarge(wl_ref[...], kl_ref)
    enlarge(wr_ref[...], kr_ref)


def far_ops_body(a_ref, own_ref, b_ref, at_ref):
    for j in range(2):
        values = a_ref[j].astype(F32)
        for p in range(2):
            b_ref[j, p] = spread(values[:, p * BLK : (p + 1) * BLK], p)
        at_ref[j, :, :128] = own_ref[j]
        at_ref[j, :, 128:] = flipped(values, 2)


def raw_tile(ref, w, lt):
    cols = slice(w * BLK, (w + 1) * BLK)
    return jnp.concatenate(
        [ref[2 * lt, :, cols].astype(F32), ref[2 * lt + 1, :, cols].astype(F32)], axis=1
    )


def flat_tile(ref, w, lt):
    at = lt * HALF + w * 128
    return ref[:, at : at + 128].astype(F32)


def grouped(ref, tile, m_ref):
    for lt in range(2):
        for u in range(9):
            first = tile(ref, 2 * u, lt).reshape(GROUPS, 8, 128)
            if 2 * u + 1 < WB:
                second = tile(ref, 2 * u + 1, lt).reshape(GROUPS, 8, 128)
            else:
                second = jnp.zeros((GROUPS, 8, 128), F32)
            both = jnp.concatenate([first, second], axis=1).astype(BF)
            m_ref[:, u * 16 : (u + 1) * 16, lt * 128 : (lt + 1) * 128] = both


def mixed(m_ref, k, count, f_ref):
    for h in range(4):
        low = dot(k, m_ref[2 * h]).reshape(count * WB, 8, 256)
        high = dot(k, m_ref[2 * h + 1]).reshape(count * WB, 8, 256)
        f_ref[:, h * 16 : (h + 1) * 16, :] = jnp.concatenate([low, high], axis=1).astype(BF)


def columns(f_ref, at, b, turned, y_ref, to):
    source = f_ref[at * WB : (at + 1) * WB].reshape(WB * BLK, 256)
    out = (dot_t(source, b) if turned else dot(source, b)).astype(BF)
    for v in range(WB):
        for lt in range(2):
            y_ref[to * BLK : (to + 1) * BLK, lt * HALF + v * 128 : lt * HALF + (v + 1) * 128] = out[
                v * BLK : (v + 1) * BLK, lt * 128 : (lt + 1) * 128
            ]


def half_body(tile, turned, flat, env_ref, k_ref, b_ref, y_ref, *rest):
    if flat:
        flat_ref, m_ref, f_ref = rest
        for lt in range(2):
            for w in range(WB):
                at = lt * HALF + w * 128
                flat_ref[:, at : at + 128] = tile(env_ref, w, lt).astype(BF)
    else:
        m_ref, f_ref = rest
    grouped(env_ref, tile, m_ref)
    mixed(m_ref, k_ref[: 2 * WB * 8], 2, f_ref)
    for p in range(2):
        columns(f_ref, p, b_ref[p], turned, y_ref, p)


def own_half(env, k, b, turned, raw):
    outs = [shape((128, FULL))]
    if raw:
        outs.append(shape((BLK, FULL)))
    return call(
        functools.partial(half_body, raw_tile if raw else flat_tile, turned, raw),
        outs,
        [pltpu.VMEM((GROUPS, DEPTH, 256), BF), pltpu.VMEM((2 * WB, BLK, 256), BF)],
        operands=(env, k, b),
        flops=1_200_000_000,
    )


def full_body(tile, turned, far_at, env_ref, k_ref, b_ref, own_ref, lhs_ref, out_ref, y_ref, m_ref, f_ref):
    y_ref[:128, :] = own_ref[...]
    grouped(env_ref, tile, m_ref)
    mixed(m_ref, k_ref[2 * WB * 8 :], 2, f_ref)
    for p in range(2):
        columns(f_ref, p, b_ref[far_at + p], turned, y_ref, 2 + p)
    low = (iota((BLK, HALF), 1) & 127) < BLK
    for lt in range(2):
        both = dot(lhs_ref[lt * 128 : (lt + 1) * 128, :], y_ref[:, lt * HALF : (lt + 1) * HALF])
        out_ref[:, lt * HALF : (lt + 1) * HALF] = jnp.where(low, both[:BLK], both[BLK:]).astype(BF)


def full_update(env, k, b, own, lhs, turned, raw, far_at):
    return call(
        functools.partial(full_body, raw_tile if raw else flat_tile, turned, far_at),
        [shape((BLK, FULL)), shape((256, FULL))],
        [pltpu.VMEM((GROUPS, DEPTH, 256), BF), pltpu.VMEM((2 * WB, BLK, 256), BF)],
        operands=(env, k, b, own, lhs),
        flops=2_400_000_000,
    )


def diagonal(ref, lt, g_ref):
    lane = (iota((BLK, HALF), 1) & 127) < BLK
    low = jnp.where(lane, 1.0, 0.0).astype(BF)
    high = jnp.where(lane, 0.0, 1.0).astype(BF)
    values = ref[:, lt * HALF : (lt + 1) * HALF]
    g_ref[:BLK, :] = values * low
    g_ref[BLK:, :] = values * high


def first_body(flag_ref, got_ref, edge_ref, k_ref, b_ref, right_ref, far_ref, out_ref, m_ref, f_ref, y_ref, g_ref):
    @pl.when(flag_ref[0] == 0)
    def _():
        grouped(got_ref, flat_tile, m_ref)

    @pl.when(flag_ref[0] != 0)
    def _():
        grouped(edge_ref, flat_tile, m_ref)

    mixed(m_ref, k_ref[...], 4, f_ref)
    for p in range(PHYS):
        columns(f_ref, p, b_ref[p], False, y_ref, p)
    for lt in range(2):
        for half, source in ((0, right_ref), (1, far_ref)):
            diagonal(source, lt, g_ref)
            out_ref[half * 128 : (half + 1) * 128, lt * 128 : (lt + 1) * 128] = dot_t(
                y_ref[half * 128 : (half + 1) * 128, lt * HALF : (lt + 1) * HALF], g_ref[...]
            )


def second_body(flag_ref, got_ref, edge_ref, y_ref, first_ref, own_ref, away_ref, sums_ref, g_ref, r_ref):
    @pl.when(flag_ref[0] == 0)
    def _():
        r_ref[...] = got_ref[...]

    @pl.when(flag_ref[0] != 0)
    def _():
        r_ref[...] = edge_ref[...]

    squares = jnp.zeros((8, 128), F32)
    for lt in range(2):
        diagonal(r_ref, lt, g_ref)
        out = dot_t(y_ref[:, lt * HALF : (lt + 1) * HALF], g_ref[...])
        own_ref[:, lt * 128 : (lt + 1) * 128] = out[:128]
        away_ref[:, lt * 128 : (lt + 1) * 128] = out[128:]
        squares = squares + jnp.sum((out * out).reshape(32, 8, 128), axis=0)
    first = first_ref[...]
    sums = jnp.sum((first * first).reshape(32, 8, 256), axis=0)
    total_first = jnp.sum(sums)
    total_second = jnp.sum(squares)
    both = jnp.where(iota((16, 8, 128), 1) < 4, total_first, total_second)
    sums_ref[...] = both


def final_body(entries, first_ref, own_ref, away_ref, sums_ref, out_ref):
    total = jnp.sum(sums_ref[...], axis=0)
    scale = lax.rsqrt(total * (1.0 / entries) + 1e-06)
    for j in range(2):
        factor = scale[4 * j : 4 * j + 1, :1]
        for s in range(4):
            parts = []
            for p in range(PHYS):
                t = target(s, p)
                if j == 0:
                    ref, at = first_ref, p * BLK
                elif p < 2:
                    ref, at = own_ref, p * BLK
                else:
                    ref, at = away_ref, (p - 2) * BLK
                parts.append(ref[at : at + BLK, t * BLK : (t + 1) * BLK])
            out_ref[j, s] = jnp.concatenate(parts, axis=1) * factor


def passed_along(block, axis, distance):
    devices = lax.axis_size(axis)
    route = [(i, (i + distance) % devices) for i in range(devices)]
    return lax.ppermute(block, axis, route)


def shifted(value, axis, by):
    devices = lax.axis_size(axis)
    pairs = [(i, i + by) for i in range(devices) if 0 <= i + by < devices]
    return lax.ppermute(value, axis, pairs)


def local(mps, left_env, right_env, row_fill, col_fill, mpo_values, mpo_pattern):
    left_raw, right_raw = left_env[0], right_env[0]
    left_behind = passed_along(left_raw, "site", 1)
    right_ahead = passed_along(right_raw, "site", -1)
    weights = mpo_values * mpo_pattern.astype(BF)
    left_small = weights.transpose(2, 1, 0).reshape(PHYS * WB, WB)
    right_small = weights.transpose(2, 0, 1).reshape(PHYS * WB, WB)
    masked, high = call(
        mask_body,
        [shape((2, 256, 256)), shape((2, 256, 128))],
        smem=2,
        operands=(row_fill, col_fill, mps),
    )
    high_behind = passed_along(high, "site", 1)
    blocks, turned_own, k_left, k_right = call(
        own_ops_body,
        [
            shape((2, PHYS, 256, 256)),
            shape((2, 256, 128)),
            shape((4 * WB * 8, DEPTH)),
            shape((4 * WB * 8, DEPTH)),
        ],
        operands=(masked, left_small, right_small),
        flops=100_000_000,
    )
    far_blocks, turned = call(
        far_ops_body,
        [shape((2, 2, 256, 256)), shape((2, 256, 256))],
        operands=(high_behind, turned_own),
    )
    left_part, left_edge = own_half(left_raw, k_left, blocks[0], False, True)
    right_part, right_edge = own_half(right_raw, k_right, blocks[1], True, True)
    left_one, _ = full_update(
        left_behind, k_left, far_blocks[0], left_part, turned[0], False, True, 0
    )
    left_one_behind = passed_along(left_one, "site", 1)
    right_one, _ = full_update(
        right_ahead, k_right, blocks[1], right_part, masked[1], True, True, 2
    )
    right_one_ahead = passed_along(right_one, "site", -1)
    (left_part,) = own_half(left_one, k_left, blocks[1], False, False)
    (right_part,) = own_half(right_one, k_right, blocks[0], True, False)
    left_out, second_mixed = full_update(
        left_one_behind, k_left, far_blocks[1], left_part, turned[1], False, False, 0
    )
    left_got = shifted(left_out, "sector", 1)
    right_out, _ = full_update(
        right_one_ahead, k_right, blocks[0], right_part, masked[0], True, False, 2
    )
    right_got = shifted(right_out, "sector", -1)
    position = lax.axis_index("sector")
    first_flag = (position == 0).astype(jnp.int32).reshape(1)
    last_flag = (position == lax.axis_size("sector") - 1).astype(jnp.int32).reshape(1)
    first = call(
        first_body,
        shape((256, 256), F32),
        [
            pltpu.VMEM((GROUPS, DEPTH, 256), BF),
            pltpu.VMEM((4 * WB, BLK, 256), BF),
            pltpu.VMEM((256, FULL), BF),
            pltpu.VMEM((128, HALF), BF),
        ],
        smem=1,
        operands=(first_flag, left_got, left_edge, k_left, blocks[0], right_one, right_one_ahead),
        flops=3_000_000_000,
    )
    own, away, sums = call(
        second_body,
        [shape((128, 256), F32), shape((128, 256), F32), shape((16, 8, 128), F32)],
        [pltpu.VMEM((128, HALF), BF), pltpu.VMEM((BLK, FULL), BF)],
        smem=1,
        operands=(last_flag, right_got, right_edge, second_mixed, first),
        flops=1_000_000_000,
    )
    devices = lax.axis_size("site")
    gathered = lax.all_to_all(sums[:devices], "site", 0, 0, tiled=True)
    back = passed_along(away, "site", -1)
    return call(
        functools.partial(final_body, 256 * 256 * devices),
        shape((2, 4, BLK, 256), F32),
        operands=(first, own, back, gathered),
    )


def solution(mesh):
    in_specs = (
        P("sector", "site", None, None),
        P("sector", "site", None, None),
        P("sector", "site", None, None),
        P("sector", "site"),
        P("sector", "site", None),
        P(),
        P(),
    )
    out_specs = P("sector", "site", None, None)
    return jax.shard_map(local, mesh=mesh, in_specs=in_specs, out_specs=out_specs, check_vma=False)
```

```python
import functools

import jax
import jax.numpy as jnp
from jax import lax
from jax.experimental import pallas as pl
from jax.experimental.pallas import tpu as pltpu
from jax.sharding import PartitionSpec as P

BLK = 64
PHYS = 4
WB = 17
HALF = WB * 128
FULL = 2 * HALF
GROUPS = 8
DEPTH = 144
BF = jnp.bfloat16
F32 = jnp.float32


def shape(dims, dtype=BF):
    return jax.ShapeDtypeStruct(dims, dtype)


def call(body, outs, scratch=(), smem=0, hbm=0, operands=(), after=(), mib=16, us=1.20):
    spaces = [pltpu.SMEM] * smem + [pltpu.HBM] * hbm
    spaces += [pltpu.VMEM] * (len(operands) - len(spaces))
    spaces += [pl.ANY] * len(after)
    single = not isinstance(outs, (list, tuple))
    out_spec = pl.BlockSpec(memory_space=pltpu.VMEM)
    count = len(operands)

    def ordered(*refs):
        body(*refs[:count], *refs[count + len(after) :])

    return pl.pallas_call(
        ordered,
        out_shape=outs,
        in_specs=[pl.BlockSpec(memory_space=space) for space in spaces],
        out_specs=out_spec if single else [out_spec] * len(outs),
        scratch_shapes=list(scratch),
        compiler_params=pltpu.CompilerParams(vmem_limit_bytes=mib * 1024 * 1024),
        cost_estimate=pl.CostEstimate(flops=int(us * 1.1e9), bytes_accessed=1, transcendentals=0),
    )(*operands, *after)


def iota(dims, axis):
    return lax.broadcasted_iota(jnp.int32, dims, axis)


def dot(a, b):
    return lax.dot_general(a, b, (((1,), (0,)), ((), ())), preferred_element_type=F32)


def dot_t(a, b):
    return lax.dot_general(a, b, (((1,), (1,)), ((), ())), preferred_element_type=F32)


def target(s, p):
    return (s + p % 2) % 4


def keep_inside(rows_hbm, cols_hbm, mps_hbm, all_ref, high_ref, rows_ref, cols_ref, mps_ref, sems):
    pairs = ((rows_hbm, rows_ref), (cols_hbm, cols_ref), (mps_hbm, mps_ref))
    copies = [pltpu.make_async_copy(a, b, sems.at[i]) for i, (a, b) in enumerate(pairs)]
    for copy in copies:
        copy.start()
    for copy in copies:
        copy.wait()
    row = iota((BLK, 256), 0)
    col = iota((BLK, 256), 1)
    inside = col & (BLK - 1)
    for j in range(2):
        for s in range(4):
            least = jnp.where(col < 64, cols_ref[j, s, 0], cols_ref[j, s, 1])
            most = jnp.where(col < 192, cols_ref[j, s, 2], cols_ref[j, s, 3])
            limit = jnp.where(col < 128, least, most)
            keep = jnp.logical_and(row < rows_ref[j, s], inside < limit)
            kept = jnp.where(keep, mps_ref[j, s].astype(F32), 0.0).astype(BF)
            all_ref[j, s * BLK : (s + 1) * BLK, :] = kept
            high_ref[j, s * BLK : (s + 1) * BLK, :] = kept[:, 128:]


def spread(block, step):
    tiled = jnp.concatenate([block] * 4, axis=1)
    goal = ((iota((256, 256), 0) >> 6) + step) & 3
    return jnp.where(goal == (iota((256, 256), 1) >> 6), tiled, 0.0).astype(BF)


def flipped(values, states):
    turned = values.T
    rows = []
    for t in range(4):
        parts = []
        for p in range(states):
            s = (t - p % 2) % 4
            parts.append(turned[p * BLK : (p + 1) * BLK, s * BLK : (s + 1) * BLK])
        rows.append(jnp.concatenate(parts, axis=1))
    return jnp.concatenate(rows, axis=0).astype(BF)


def enlarge(small, out_ref):
    rows = 4 * WB * 8
    up = jnp.where((iota((rows, 4 * WB), 0) >> 3) == iota((rows, 4 * WB), 1), 1.0, 0.0)
    out = jnp.where((iota((WB, DEPTH), 1) >> 3) == iota((WB, DEPTH), 0), 1.0, 0.0)
    tall = dot(up.astype(BF), small).astype(BF)
    wide = dot(tall, out.astype(BF))
    same = (iota((rows, DEPTH), 0) & 7) == (iota((rows, DEPTH), 1) & 7)
    out_ref[...] = jnp.where(same, wide, 0.0).astype(BF)


def own_ops_body(a_ref, wl_ref, wr_ref, b_ref, at_ref, kl_ref, kr_ref):
    for j in range(2):
        values = a_ref[j].astype(F32)
        for p in range(PHYS):
            b_ref[j, p] = spread(values[:, p * BLK : (p + 1) * BLK], p % 2)
        at_ref[j] = flipped(values[:, :128], 2)
    enlarge(wl_ref[...], kl_ref)
    enlarge(wr_ref[...], kr_ref)


def far_ops_body(a_ref, own_ref, b_ref, at_ref):
    for j in range(2):
        values = a_ref[j].astype(F32)
        for p in range(2):
            b_ref[j, p] = spread(values[:, p * BLK : (p + 1) * BLK], p)
        at_ref[j, :, :128] = own_ref[j]
        at_ref[j, :, 128:] = flipped(values, 2)


def raw_pair(ref, u, lt):
    lane = iota((BLK, 128), 1) < BLK
    if u == WB // 2:
        cols = slice(2 * u * BLK, WB * BLK)
        parts = [ref[2 * lt + i, :, cols].astype(F32) for i in range(2)]
        return jnp.concatenate(parts, axis=1), None
    low = ref[2 * lt, :, u * 128 : (u + 1) * 128].astype(F32)
    high = ref[2 * lt + 1, :, u * 128 : (u + 1) * 128].astype(F32)
    first = jnp.where(lane, low, pltpu.roll(high, BLK, 1))
    second = jnp.where(lane, pltpu.roll(low, BLK, 1), high)
    return first, second


def flat_pair(ref, u, lt):
    at = lt * HALF + 2 * u * 128
    first = ref[:, at : at + 128].astype(F32)
    if u == WB // 2:
        return first, None
    return first, ref[:, at + 128 : at + 256].astype(F32)


def flatten(env_ref, flat_ref):
    for lt in range(2):
        for u in range(9):
            at = lt * HALF + 2 * u * 128
            first, second = raw_pair(env_ref, u, lt)
            flat_ref[:, at : at + 128] = first.astype(BF)
            if second is not None:
                flat_ref[:, at + 128 : at + 256] = second.astype(BF)


def rows_of(flat_ref, e_ref):
    for lt in range(2):
        for w in range(WB):
            at = lt * HALF + w * 128
            e_ref[w * BLK : (w + 1) * BLK, lt * 128 : (lt + 1) * 128] = flat_ref[:, at : at + 128]


def woven(first, second):
    width = first.shape[-1]
    if second is None:
        second = jnp.zeros_like(first)
    parts = [first.reshape(GROUPS, 8, width), second.reshape(GROUPS, 8, width)]
    return jnp.concatenate(parts, axis=1).astype(BF)


def grouped(ref, m_ref):
    for lt in range(2):
        for u in range(9):
            both = woven(*flat_pair(ref, u, lt))
            m_ref[:, u * 16 : (u + 1) * 16, lt * 128 : (lt + 1) * 128] = both


def mixed(m_ref, k, count, h):
    low = dot(k, m_ref[2 * h]).reshape(count * WB, 8, 256)
    high = dot(k, m_ref[2 * h + 1]).reshape(count * WB, 8, 256)
    return jnp.concatenate([low, high], axis=1).astype(BF)


def left_states(e_ref, k_ref, k_at, b_ref, states, m_ref, y_ref, to):
    for p in range(states):
        inner = dot(e_ref[...], b_ref[p])
        for u in range(9):
            first = inner[2 * u * BLK : (2 * u + 1) * BLK]
            second = inner[(2 * u + 1) * BLK : (2 * u + 2) * BLK] if 2 * u + 1 < WB else None
            m_ref[p, :, u * 16 : (u + 1) * 16, :] = woven(first, second)
        k = k_ref[(k_at + p) * WB * 8 : (k_at + p + 1) * WB * 8]
        for h in range(4):
            out = mixed(m_ref.at[p], k, 1, h)
            rows = slice((to + p) * BLK + h * 16, (to + p) * BLK + (h + 1) * 16)
            for v in range(WB):
                for lt in range(2):
                    y_ref[rows, lt * HALF + v * 128 : lt * HALF + (v + 1) * 128] = out[
                        v, :, lt * 128 : (lt + 1) * 128
                    ]


def right_states(m_ref, k, b_ref, b_at, f_ref, y_ref, to):
    for h in range(4):
        f_ref[:, h * 16 : (h + 1) * 16, :] = mixed(m_ref, k, 2, h)
    for p in range(2):
        source = f_ref[p * WB : (p + 1) * WB].reshape(WB * BLK, 256)
        out = dot_t(source, b_ref[b_at + p]).astype(BF)
        rows = slice((to + p) * BLK, (to + p + 1) * BLK)
        for v in range(WB):
            for lt in range(2):
                y_ref[rows, lt * HALF + v * 128 : lt * HALF + (v + 1) * 128] = out[
                    v * BLK : (v + 1) * BLK, lt * 128 : (lt + 1) * 128
                ]


def closed(lhs_ref, own_ref, y_ref, out_ref):
    low = (iota((BLK, HALF), 1) & 127) < BLK
    for lt in range(2):
        cols = slice(lt * HALF, (lt + 1) * HALF)
        inner = jnp.concatenate([own_ref[:, cols], y_ref[:, cols]], axis=0)
        both = dot(lhs_ref[lt * 128 : (lt + 1) * 128, :], inner)
        out_ref[:, cols] = jnp.where(low, both[:BLK], both[BLK:]).astype(BF)


def left_half(flat_ref, k_ref, b_ref, y_ref, e_ref, m_ref):
    rows_of(flat_ref, e_ref)
    left_states(e_ref, k_ref, 0, b_ref, 2, m_ref, y_ref, 0)


def right_half(flat_ref, k_ref, b_ref, y_ref, m_ref, f_ref):
    grouped(flat_ref, m_ref)
    right_states(m_ref, k_ref[: 2 * WB * 8], b_ref, 0, f_ref, y_ref, 0)


def left_rest_raw(env_ref, k_ref, b_ref, own_ref, lhs_ref, out_ref, flat_ref, y_ref, e_ref, m_ref):
    flatten(env_ref, flat_ref)
    left_rest(flat_ref, k_ref, b_ref, own_ref, lhs_ref, out_ref, y_ref, e_ref, m_ref)


def left_rest(flat_ref, k_ref, b_ref, own_ref, lhs_ref, out_ref, y_ref, e_ref, m_ref):
    rows_of(flat_ref, e_ref)
    left_states(e_ref, k_ref, 2, b_ref, 2, m_ref, y_ref, 0)
    closed(lhs_ref, own_ref, y_ref, out_ref)


def right_rest_raw(env_ref, k_ref, b_ref, own_ref, lhs_ref, out_ref, flat_ref, y_ref, m_ref, f_ref):
    flatten(env_ref, flat_ref)
    right_rest(flat_ref, k_ref, b_ref, own_ref, lhs_ref, out_ref, y_ref, m_ref, f_ref)


def right_rest(flat_ref, k_ref, b_ref, own_ref, lhs_ref, out_ref, y_ref, m_ref, f_ref):
    grouped(flat_ref, m_ref)
    right_states(m_ref, k_ref[2 * WB * 8 :], b_ref, 2, f_ref, y_ref, 0)
    closed(lhs_ref, own_ref, y_ref, out_ref)


def prepare(left_hbm, right_hbm, a_ref, wl_ref, wr_ref, b_ref, at_ref, kl_ref, kr_ref, yl_ref, yr_ref, fl_ref, fr_ref, raw_ref, e_ref, m_ref, g_ref, f_ref, sems):
    copies = [
        pltpu.make_async_copy(source, raw_ref.at[i], sems.at[i])
        for i, source in enumerate((left_hbm, right_hbm))
    ]
    for copy in copies:
        copy.start()
    own_ops_body(a_ref, wl_ref, wr_ref, b_ref, at_ref, kl_ref, kr_ref)
    copies[0].wait()
    flatten(raw_ref.at[0], fl_ref)
    left_half(fl_ref, kl_ref, b_ref.at[0], yl_ref, e_ref, m_ref)
    copies[1].wait()
    flatten(raw_ref.at[1], fr_ref)
    right_half(fr_ref, kr_ref, b_ref.at[1], yr_ref, g_ref, f_ref)


LEFT_SCRATCH = [pltpu.VMEM((WB * BLK, 256), BF), pltpu.VMEM((2, GROUPS, DEPTH, 256), BF)]
RIGHT_SCRATCH = [pltpu.VMEM((GROUPS, DEPTH, 256), BF), pltpu.VMEM((2 * WB, BLK, 256), BF)]


def diagonal(ref, lt, g_ref):
    lane = (iota((BLK, HALF), 1) & 127) < BLK
    low = jnp.where(lane, 1.0, 0.0).astype(BF)
    high = jnp.where(lane, 0.0, 1.0).astype(BF)
    values = ref[:, lt * HALF : (lt + 1) * HALF]
    g_ref[:BLK, :] = values * low
    g_ref[BLK:, :] = values * high


def chosen(flag_ref, got_ref, edge_ref, g_ref):
    @pl.when(flag_ref[0] == 0)
    def _():
        for lt in range(2):
            diagonal(got_ref, lt, g_ref.at[lt])

    @pl.when(flag_ref[0] != 0)
    def _():
        for lt in range(2):
            diagonal(edge_ref, lt, g_ref.at[lt])


def squared(values):
    return jnp.sum((values * values).reshape(-1, 8, values.shape[1]), axis=0)


def first_body(flag_ref, got_ref, edge_ref, own_ref, far_ref, out_ref, sum_ref, g_ref):
    chosen(flag_ref, got_ref, edge_ref, g_ref)
    total = jnp.zeros((8, 256), F32)
    for lt in range(2):
        cols = slice(lt * HALF, (lt + 1) * HALF)
        inner = jnp.concatenate([own_ref[:, cols], far_ref[:, cols]], axis=0)
        out = dot_t(g_ref[lt], inner)
        out_ref[lt * 128 : (lt + 1) * 128, :] = out
        total = total + squared(out)
    sum_ref[...] = total[:, :128] + total[:, 128:]


def second_body(flag_ref, got_ref, edge_ref, y_ref, far_ref, sum_ref, own_ref, away_ref, sums_ref, g_ref):
    chosen(flag_ref, got_ref, edge_ref, g_ref)
    total = jnp.zeros((8, 128), F32)
    for lt in range(2):
        cols = slice(lt * HALF, (lt + 1) * HALF)
        inner = jnp.concatenate([y_ref[:, cols], far_ref[:, cols]], axis=0)
        out = dot_t(inner, g_ref[lt])
        own_ref[:, lt * 128 : (lt + 1) * 128] = out[:128]
        away_ref[:, lt * 128 : (lt + 1) * 128] = out[128:]
        total = total + squared(out)
    first = jnp.sum(sum_ref[...])
    sums_ref[...] = jnp.where(iota(sums_ref.shape, 1) < 4, first, jnp.sum(total))


def final_body(entries, first_ref, own_ref, away_ref, sums_ref, out_ref):
    total = jnp.sum(sums_ref[...], axis=0)
    scale = lax.rsqrt(total * (1.0 / entries) + 1e-06)
    for s in range(4):
        out_ref[0, s] = first_ref[s * BLK : (s + 1) * BLK, :] * scale[:1, :1]
        parts = []
        for p in range(PHYS):
            ref, at = (own_ref, p) if p < 2 else (away_ref, p - 2)
            t = target(s, p)
            parts.append(ref[at * BLK : (at + 1) * BLK, t * BLK : (t + 1) * BLK])
        out_ref[1, s] = jnp.concatenate(parts, axis=1) * scale[4:5, :1]


def passed_along(block, axis, distance):
    devices = lax.axis_size(axis)
    route = [(i, (i + distance) % devices) for i in range(devices)]
    return lax.ppermute(block, axis, route)


def shifted(value, axis, by):
    devices = lax.axis_size(axis)
    pairs = [(i, i + by) for i in range(devices) if 0 <= i + by < devices]
    return lax.ppermute(value, axis, pairs)


def local(mps, left_env, right_env, row_fill, col_fill, mpo_values, mpo_pattern):
    left_raw, right_raw = left_env[0], right_env[0]
    left_behind = passed_along(left_raw, "site", 1)
    right_ahead = passed_along(right_raw, "site", -1)
    weights = mpo_values * mpo_pattern.astype(BF)
    left_small = weights.transpose(2, 1, 0).reshape(PHYS * WB, WB)
    right_small = weights.transpose(2, 0, 1).reshape(PHYS * WB, WB)
    masked, high = call(
        keep_inside,
        [shape((2, 256, 256)), shape((2, 256, 128))],
        [
            pltpu.SMEM((2, 4), jnp.int32),
            pltpu.SMEM((2, 4, PHYS), jnp.int32),
            pltpu.VMEM((2, 4, BLK, 256), BF),
            pltpu.SemaphoreType.DMA((3,)),
        ],
        hbm=3,
        operands=(row_fill, col_fill, mps),
        mib=58,
    )
    high_behind = passed_along(high, "site", 1)
    rows = 4 * WB * 8
    part, flat = shape((128, FULL)), shape((BLK, FULL))
    blocks, turned_own, k_left, k_right, left_part, right_part, left_edge, right_edge = call(
        prepare,
        [
            shape((2, PHYS, 256, 256)),
            shape((2, 256, 128)),
            shape((rows, DEPTH)),
            shape((rows, DEPTH)),
            part,
            part,
            flat,
            flat,
        ],
        [
            pltpu.VMEM((2, 4, BLK, WB * BLK), BF),
            *LEFT_SCRATCH,
            *RIGHT_SCRATCH,
            pltpu.SemaphoreType.DMA((2,)),
        ],
        hbm=2,
        operands=(left_raw, right_raw, masked, left_small, right_small),
        mib=16,
    )
    whole = pltpu.VMEM((128, FULL), BF)
    kept = pltpu.VMEM((BLK, FULL), BF)
    far_blocks, turned = call(
        far_ops_body,
        [shape((2, 2, 256, 256)), shape((2, 256, 256))],
        operands=(high_behind, turned_own),
        after=(left_part, right_part, left_behind, right_ahead),
    )
    left_one = call(
        left_rest_raw,
        flat,
        [kept, whole, *LEFT_SCRATCH],
        operands=(left_behind, k_left, far_blocks[0], left_part, turned[0]),
        after=(right_part,),
    )
    left_one_behind = passed_along(left_one, "site", 1)
    right_one = call(
        right_rest_raw,
        flat,
        [kept, whole, *RIGHT_SCRATCH],
        operands=(right_ahead, k_right, blocks[1], right_part, masked[1]),
        after=(left_one,),
    )
    right_one_ahead = passed_along(right_one, "site", -1)
    left_part = call(
        left_half, part, LEFT_SCRATCH, operands=(left_one, k_left, blocks[1]), after=(right_one,)
    )
    right_part = call(right_half, part, RIGHT_SCRATCH, operands=(right_one, k_right, blocks[0]))
    left_out, left_far = call(
        left_rest,
        [flat, part],
        LEFT_SCRATCH,
        operands=(left_one_behind, k_left, far_blocks[1], left_part, turned[1]),
        after=(right_part,),
    )
    left_got = shifted(left_out, "sector", 1)
    right_out, right_far = call(
        right_rest,
        [flat, part],
        RIGHT_SCRATCH,
        operands=(right_one_ahead, k_right, blocks[0], right_part, masked[0]),
        after=(left_out,),
    )
    right_got = shifted(right_out, "sector", -1)
    position = lax.axis_index("sector")
    first_flag = (position == 0).astype(jnp.int32).reshape(1)
    last_flag = (position == lax.axis_size("sector") - 1).astype(jnp.int32).reshape(1)
    diag = pltpu.VMEM((2, 128, HALF), BF)
    first, first_sum = call(
        first_body,
        [shape((256, 256), F32), shape((8, 128), F32)],
        [diag],
        smem=1,
        operands=(first_flag, left_got, left_edge, right_part, right_far),
        after=(right_out,),
    )
    devices = lax.axis_size("site")
    own, away, sums = call(
        second_body,
        [shape((128, 256), F32), shape((128, 256), F32), shape((devices, 8, 128), F32)],
        [diag],
        smem=1,
        operands=(last_flag, right_got, right_edge, left_part, left_far, first_sum),
    )
    back = passed_along(away, "site", -1)
    gathered = lax.all_to_all(sums, "site", 0, 0, tiled=True)
    return call(
        functools.partial(final_body, 256 * 256 * devices),
        shape((2, 4, BLK, 256), F32),
        operands=(first, own, back, gathered),
    )


def solution(mesh):
    in_specs = (
        P("sector", "site", None, None),
        P("sector", "site", None, None),
        P("sector", "site", None, None),
        P("sector", "site"),
        P("sector", "site", None),
        P(),
        P(),
    )
    out_specs = P("sector", "site", None, None)
    return jax.shard_map(local, mesh=mesh, in_specs=in_specs, out_specs=out_specs, check_vma=False)
```

```python
import functools

import jax
import jax.numpy as jnp
from jax import lax
from jax.experimental import pallas as pl
from jax.experimental.pallas import tpu as pltpu
from jax.sharding import PartitionSpec as P

BLK = 64
PHYS = 4
WB = 17
HALF = WB * 128
FULL = 2 * HALF
GROUPS = 8
DEPTH = 144
BF = jnp.bfloat16
F32 = jnp.float32


def shape(dims, dtype=BF):
    return pltpu.VMEM(dims, dtype)


def call(body, outs, scratch=(), smem=0, hbm=0, operands=(), after=(), mib=16, us=1.20):
    spaces = [pltpu.SMEM] * smem + [pltpu.HBM] * hbm
    spaces += [pltpu.VMEM] * (len(operands) - len(spaces))
    spaces += [pl.ANY] * len(after)
    single = not isinstance(outs, (list, tuple))
    out_specs = [
        pl.BlockSpec(memory_space=pltpu.HBM if getattr(out, "memory_space", None) == pltpu.HBM else pltpu.VMEM)
        for out in ([outs] if single else outs)
    ]
    count = len(operands)
    placed = [
        pltpu.with_memory_space_constraint(value, space) if space == pltpu.HBM else value
        for value, space in zip(operands, spaces)
    ]

    def ordered(*refs):
        body(*refs[:count], *refs[count + len(after) :])

    return pl.pallas_call(
        ordered,
        out_shape=outs,
        in_specs=[pl.BlockSpec(memory_space=space) for space in spaces],
        out_specs=out_specs[0] if single else out_specs,
        scratch_shapes=list(scratch),
        compiler_params=pltpu.CompilerParams(vmem_limit_bytes=mib * 1024 * 1024),
        cost_estimate=pl.CostEstimate(flops=int(us * 1.1e9), bytes_accessed=1, transcendentals=0),
    )(*placed, *after)


def iota(dims, axis):
    return lax.broadcasted_iota(jnp.int32, dims, axis)


def dot(a, b):
    return lax.dot_general(a, b, (((1,), (0,)), ((), ())), preferred_element_type=F32)


def dot_t(a, b):
    return lax.dot_general(a, b, (((1,), (1,)), ((), ())), preferred_element_type=F32)


def target(s, p):
    return (s + p % 2) % 4


def keep_inside(rows_hbm, cols_hbm, mps_hbm, all_ref, high_ref, rows_ref, cols_ref, mps_ref, sems):
    pairs = ((rows_hbm, rows_ref), (cols_hbm, cols_ref), (mps_hbm, mps_ref))
    copies = [pltpu.make_async_copy(a, b, sems.at[i]) for i, (a, b) in enumerate(pairs)]
    for copy in copies:
        copy.start()
    for copy in copies:
        copy.wait()
    row = iota((BLK, 256), 0)
    col = iota((BLK, 256), 1)
    inside = col & (BLK - 1)
    for j in range(2):
        for s in range(4):
            least = jnp.where(col < 64, cols_ref[j, s, 0], cols_ref[j, s, 1])
            most = jnp.where(col < 192, cols_ref[j, s, 2], cols_ref[j, s, 3])
            limit = jnp.where(col < 128, least, most)
            keep = jnp.logical_and(row < rows_ref[j, s], inside < limit)
            kept = jnp.where(keep, mps_ref[j, s].astype(F32), 0.0).astype(BF)
            all_ref[j, s * BLK : (s + 1) * BLK, :] = kept
            high_ref[j, s * BLK : (s + 1) * BLK, :] = kept[:, 128:]


def spread(block, step):
    tiled = jnp.concatenate([block] * 4, axis=1)
    goal = ((iota((256, 256), 0) >> 6) + step) & 3
    return jnp.where(goal == (iota((256, 256), 1) >> 6), tiled, 0.0).astype(BF)


def flipped(values, states):
    turned = values.T
    rows = []
    for t in range(4):
        parts = []
        for p in range(states):
            s = (t - p % 2) % 4
            parts.append(turned[p * BLK : (p + 1) * BLK, s * BLK : (s + 1) * BLK])
        rows.append(jnp.concatenate(parts, axis=1))
    return jnp.concatenate(rows, axis=0).astype(BF)


def enlarge(small, out_ref):
    rows = 4 * WB * 8
    up = jnp.where((iota((rows, 4 * WB), 0) >> 3) == iota((rows, 4 * WB), 1), 1.0, 0.0)
    out = jnp.where((iota((WB, DEPTH), 1) >> 3) == iota((WB, DEPTH), 0), 1.0, 0.0)
    tall = dot(up.astype(BF), small).astype(BF)
    wide = dot(tall, out.astype(BF))
    same = (iota((rows, DEPTH), 0) & 7) == (iota((rows, DEPTH), 1) & 7)
    out_ref[...] = jnp.where(same, wide, 0.0).astype(BF)


def own_ops_body(a_ref, wl_ref, wr_ref, b_ref, at_ref, kl_ref, kr_ref):
    for j in range(2):
        values = a_ref[j].astype(F32)
        for p in range(PHYS):
            b_ref[j, p] = spread(values[:, p * BLK : (p + 1) * BLK], p % 2)
        at_ref[j] = flipped(values[:, :128], 2)
    enlarge(wl_ref[...], kl_ref)
    enlarge(wr_ref[...], kr_ref)


def far_ops_body(a_ref, own_ref, b_ref, at_ref):
    for j in range(2):
        values = a_ref[j].astype(F32)
        for p in range(2):
            b_ref[j, p] = spread(values[:, p * BLK : (p + 1) * BLK], p)
        at_ref[j, :, :128] = own_ref[j]
        at_ref[j, :, 128:] = flipped(values, 2)


def raw_pair(ref, u, lt):
    lane = iota((BLK, 128), 1) < BLK
    if u == WB // 2:
        cols = slice(2 * u * BLK, WB * BLK)
        parts = [ref[2 * lt + i, :, cols].astype(F32) for i in range(2)]
        return jnp.concatenate(parts, axis=1), None
    low = ref[2 * lt, :, u * 128 : (u + 1) * 128].astype(F32)
    high = ref[2 * lt + 1, :, u * 128 : (u + 1) * 128].astype(F32)
    first = jnp.where(lane, low, pltpu.roll(high, BLK, 1))
    second = jnp.where(lane, pltpu.roll(low, BLK, 1), high)
    return first, second


def flat_pair(ref, u, lt):
    at = lt * HALF + 2 * u * 128
    first = ref[:, at : at + 128].astype(F32)
    if u == WB // 2:
        return first, None
    return first, ref[:, at + 128 : at + 256].astype(F32)


def flatten(env_ref, flat_ref):
    for lt in range(2):
        for u in range(9):
            at = lt * HALF + 2 * u * 128
            first, second = raw_pair(env_ref, u, lt)
            flat_ref[:, at : at + 128] = first.astype(BF)
            if second is not None:
                flat_ref[:, at + 128 : at + 256] = second.astype(BF)


def rows_of(flat_ref, e_ref):
    for lt in range(2):
        for w in range(WB):
            at = lt * HALF + w * 128
            e_ref[w * BLK : (w + 1) * BLK, lt * 128 : (lt + 1) * 128] = flat_ref[:, at : at + 128]


def woven(first, second):
    width = first.shape[-1]
    if second is None:
        second = jnp.zeros_like(first)
    parts = [first.reshape(GROUPS, 8, width), second.reshape(GROUPS, 8, width)]
    return jnp.concatenate(parts, axis=1).astype(BF)


def grouped(ref, m_ref):
    for lt in range(2):
        for u in range(9):
            both = woven(*flat_pair(ref, u, lt))
            m_ref[:, u * 16 : (u + 1) * 16, lt * 128 : (lt + 1) * 128] = both


def mixed(m_ref, k, count, h):
    low = dot(k, m_ref[2 * h]).reshape(count * WB, 8, 256)
    high = dot(k, m_ref[2 * h + 1]).reshape(count * WB, 8, 256)
    return jnp.concatenate([low, high], axis=1).astype(BF)


def left_states(e_ref, k_ref, k_at, b_ref, states, m_ref, y_ref, to):
    for p in range(states):
        inner = dot(e_ref[...], b_ref[p])
        for u in range(9):
            first = inner[2 * u * BLK : (2 * u + 1) * BLK]
            second = inner[(2 * u + 1) * BLK : (2 * u + 2) * BLK] if 2 * u + 1 < WB else None
            m_ref[p, :, u * 16 : (u + 1) * 16, :] = woven(first, second)
        k = k_ref[(k_at + p) * WB * 8 : (k_at + p + 1) * WB * 8]
        for h in range(4):
            out = mixed(m_ref.at[p], k, 1, h)
            rows = slice((to + p) * BLK + h * 16, (to + p) * BLK + (h + 1) * 16)
            for v in range(WB):
                for lt in range(2):
                    y_ref[rows, lt * HALF + v * 128 : lt * HALF + (v + 1) * 128] = out[
                        v, :, lt * 128 : (lt + 1) * 128
                    ]


def right_states(m_ref, k, b_ref, b_at, f_ref, y_ref, to):
    for h in range(4):
        f_ref[:, h * 16 : (h + 1) * 16, :] = mixed(m_ref, k, 2, h)
    for p in range(2):
        source = f_ref[p * WB : (p + 1) * WB].reshape(WB * BLK, 256)
        out = dot_t(source, b_ref[b_at + p]).astype(BF)
        rows = slice((to + p) * BLK, (to + p + 1) * BLK)
        for v in range(WB):
            for lt in range(2):
                y_ref[rows, lt * HALF + v * 128 : lt * HALF + (v + 1) * 128] = out[
                    v * BLK : (v + 1) * BLK, lt * 128 : (lt + 1) * 128
                ]


def closed(lhs_ref, own_ref, y_ref, out_ref):
    low = (iota((BLK, HALF), 1) & 127) < BLK
    for lt in range(2):
        cols = slice(lt * HALF, (lt + 1) * HALF)
        inner = jnp.concatenate([own_ref[:, cols], y_ref[:, cols]], axis=0)
        both = dot(lhs_ref[lt * 128 : (lt + 1) * 128, :], inner)
        out_ref[:, cols] = jnp.where(low, both[:BLK], both[BLK:]).astype(BF)


def left_half(flat_ref, k_ref, b_ref, y_ref, e_ref, m_ref):
    rows_of(flat_ref, e_ref)
    left_states(e_ref, k_ref, 0, b_ref, 2, m_ref, y_ref, 0)


def right_half(flat_ref, k_ref, b_ref, y_ref, m_ref, f_ref):
    grouped(flat_ref, m_ref)
    right_states(m_ref, k_ref[: 2 * WB * 8], b_ref, 0, f_ref, y_ref, 0)


def left_rest_raw(env_ref, k_ref, b_ref, own_ref, lhs_ref, out_ref, flat_ref, y_ref, e_ref, m_ref):
    flatten(env_ref, flat_ref)
    left_rest(flat_ref, k_ref, b_ref, own_ref, lhs_ref, out_ref, y_ref, e_ref, m_ref)


def left_rest(flat_ref, k_ref, b_ref, own_ref, lhs_ref, out_ref, y_ref, e_ref, m_ref):
    rows_of(flat_ref, e_ref)
    left_states(e_ref, k_ref, 2, b_ref, 2, m_ref, y_ref, 0)
    closed(lhs_ref, own_ref, y_ref, out_ref)


def right_rest_raw(env_ref, k_ref, b_ref, own_ref, lhs_ref, out_ref, flat_ref, y_ref, m_ref, f_ref):
    flatten(env_ref, flat_ref)
    right_rest(flat_ref, k_ref, b_ref, own_ref, lhs_ref, out_ref, y_ref, m_ref, f_ref)


def right_rest(flat_ref, k_ref, b_ref, own_ref, lhs_ref, out_ref, y_ref, m_ref, f_ref):
    grouped(flat_ref, m_ref)
    right_states(m_ref, k_ref[2 * WB * 8 :], b_ref, 2, f_ref, y_ref, 0)
    closed(lhs_ref, own_ref, y_ref, out_ref)


def prepare(left_hbm, right_hbm, a_ref, wl_ref, wr_ref, b_ref, at_ref, kl_ref, kr_ref, yl_ref, yr_ref, raw_ref, flat_ref, e_ref, m_ref, g_ref, f_ref, sems):
    copies = [
        pltpu.make_async_copy(source, raw_ref.at[i], sems.at[i])
        for i, source in enumerate((left_hbm, right_hbm))
    ]
    for copy in copies:
        copy.start()
    own_ops_body(a_ref, wl_ref, wr_ref, b_ref, at_ref, kl_ref, kr_ref)
    copies[0].wait()
    flatten(raw_ref.at[0], flat_ref.at[0])
    left_half(flat_ref.at[0], kl_ref, b_ref.at[0], yl_ref, e_ref, m_ref)
    copies[1].wait()
    flatten(raw_ref.at[1], flat_ref.at[1])
    right_half(flat_ref.at[1], kr_ref, b_ref.at[1], yr_ref, g_ref, f_ref)


LEFT_SCRATCH = [pltpu.VMEM((WB * BLK, 256), BF), pltpu.VMEM((2, GROUPS, DEPTH, 256), BF)]
RIGHT_SCRATCH = [pltpu.VMEM((GROUPS, DEPTH, 256), BF), pltpu.VMEM((2 * WB, BLK, 256), BF)]


def diagonal(ref, lt, g_ref):
    lane = (iota((BLK, HALF), 1) & 127) < BLK
    low = jnp.where(lane, 1.0, 0.0).astype(BF)
    high = jnp.where(lane, 0.0, 1.0).astype(BF)
    values = ref[:, lt * HALF : (lt + 1) * HALF]
    g_ref[:BLK, :] = values * low
    g_ref[BLK:, :] = values * high


def chosen(flag_ref, edge_hbm, got_ref, raw_ref, flat_ref, g_ref, sem):
    @pl.when(flag_ref[0] == 0)
    def _():
        for lt in range(2):
            diagonal(got_ref, lt, g_ref.at[lt])

    @pl.when(flag_ref[0] != 0)
    def _():
        fetched = pltpu.make_async_copy(edge_hbm, raw_ref, sem)
        fetched.start()
        fetched.wait()
        flatten(raw_ref, flat_ref)
        for lt in range(2):
            diagonal(flat_ref, lt, g_ref.at[lt])


def squared(values):
    return jnp.sum((values * values).reshape(-1, 8, values.shape[1]), axis=0)


def first_body(flag_ref, edge_hbm, got_ref, own_ref, far_ref, sum_ref, out_ref, sums_ref, raw_ref, flat_ref, g_ref, sem):
    chosen(flag_ref, edge_hbm, got_ref, raw_ref, flat_ref, g_ref, sem)
    total = jnp.zeros((8, 256), F32)
    for lt in range(2):
        cols = slice(lt * HALF, (lt + 1) * HALF)
        inner = jnp.concatenate([own_ref[:, cols], far_ref[:, cols]], axis=0)
        out = dot_t(g_ref[lt], inner)
        out_ref[lt * 128 : (lt + 1) * 128, :] = out
        total = total + squared(out)
    second = jnp.sum(sum_ref[...])
    sums_ref[...] = jnp.where(iota(sums_ref.shape, 1) < 4, jnp.sum(total), second)


def second_body(flag_ref, edge_hbm, got_ref, y_ref, far_ref, own_ref, away_ref, sum_ref, raw_ref, flat_ref, g_ref, sem):
    chosen(flag_ref, edge_hbm, got_ref, raw_ref, flat_ref, g_ref, sem)
    total = jnp.zeros((8, 128), F32)
    for lt in range(2):
        cols = slice(lt * HALF, (lt + 1) * HALF)
        inner = jnp.concatenate([y_ref[:, cols], far_ref[:, cols]], axis=0)
        out = dot_t(inner, g_ref[lt])
        own_ref[:, lt * 128 : (lt + 1) * 128] = out[:128]
        away_ref[:, lt * 128 : (lt + 1) * 128] = out[128:]
        total = total + squared(out)
    sum_ref[...] = total


def final_body(entries, first_ref, own_ref, away_ref, sums_ref, out_ref):
    total = jnp.sum(sums_ref[...], axis=0)
    scale = lax.rsqrt(total * (1.0 / entries) + 1e-06)
    for s in range(4):
        out_ref[0, s] = first_ref[s * BLK : (s + 1) * BLK, :] * scale[:1, :1]
        parts = []
        for p in range(PHYS):
            ref, at = (own_ref, p) if p < 2 else (away_ref, p - 2)
            t = target(s, p)
            parts.append(ref[at * BLK : (at + 1) * BLK, t * BLK : (t + 1) * BLK])
        out_ref[1, s] = jnp.concatenate(parts, axis=1) * scale[4:5, :1]


def passed_along(block, axis, distance):
    devices = lax.axis_size(axis)
    route = [(i, (i + distance) % devices) for i in range(devices)]
    return lax.ppermute(block, axis, route)


def shifted(value, axis, by):
    devices = lax.axis_size(axis)
    pairs = [(i, i + by) for i in range(devices) if 0 <= i + by < devices]
    return lax.ppermute(value, axis, pairs)


def local(mps, left_env, right_env, row_fill, col_fill, mpo_values, mpo_pattern):
    left_raw, right_raw = left_env[0], right_env[0]
    left_behind = passed_along(left_raw, "site", 1)
    right_ahead = passed_along(right_raw, "site", -1)
    weights = mpo_values * mpo_pattern.astype(BF)
    left_small = weights.transpose(2, 1, 0).reshape(PHYS * WB, WB)
    right_small = weights.transpose(2, 0, 1).reshape(PHYS * WB, WB)
    masked, high = call(
        keep_inside,
        [shape((2, 256, 256)), shape((2, 256, 128))],
        [
            pltpu.SMEM((2, 4), jnp.int32),
            pltpu.SMEM((2, 4, PHYS), jnp.int32),
            pltpu.VMEM((2, 4, BLK, 256), BF),
            pltpu.SemaphoreType.DMA((3,)),
        ],
        hbm=3,
        operands=(row_fill, col_fill, mps),
    )
    high_behind = passed_along(high, "site", 1)
    rows = 4 * WB * 8
    part, flat = shape((128, FULL)), shape((BLK, FULL))
    blocks, turned_own, k_left, k_right, left_part, right_part = call(
        prepare,
        [
            shape((2, PHYS, 256, 256)),
            shape((2, 256, 128)),
            shape((rows, DEPTH)),
            shape((rows, DEPTH)),
            part,
            part,
        ],
        [
            pltpu.VMEM((2, 4, BLK, WB * BLK), BF),
            pltpu.VMEM((2, BLK, FULL), BF),
            *LEFT_SCRATCH,
            *RIGHT_SCRATCH,
            pltpu.SemaphoreType.DMA((2,)),
        ],
        hbm=2,
        operands=(left_raw, right_raw, masked, left_small, right_small),
        mib=16,
    )
    whole = pltpu.VMEM((128, FULL), BF)
    kept = pltpu.VMEM((BLK, FULL), BF)
    right_one = call(
        right_rest_raw,
        flat,
        [kept, whole, *RIGHT_SCRATCH],
        operands=(right_ahead, k_right, blocks[1], right_part, masked[1]),
        after=(left_part,),
    )
    right_one_ahead = passed_along(right_one, "site", -1)
    far_blocks, turned = call(
        far_ops_body,
        [shape((2, 2, 256, 256)), shape((2, 256, 256))],
        operands=(high_behind, turned_own),
        after=(right_one, left_behind),
        us=0.4,
    )
    left_one = call(
        left_rest_raw,
        flat,
        [kept, whole, *LEFT_SCRATCH],
        operands=(left_behind, k_left, far_blocks[0], left_part, turned[0]),
        after=(right_one,),
    )
    left_one_behind = passed_along(left_one, "site", 1)
    right_part = call(
        right_half, part, RIGHT_SCRATCH, operands=(right_one, k_right, blocks[0]), after=(left_one,)
    )
    left_part = call(left_half, part, LEFT_SCRATCH, operands=(left_one, k_left, blocks[1]))
    right_out, right_far = call(
        right_rest,
        [flat, part],
        RIGHT_SCRATCH,
        operands=(right_one_ahead, k_right, blocks[0], right_part, masked[0]),
        after=(left_part,),
    )
    right_got = shifted(right_out, "sector", -1)
    left_out, left_far = call(
        left_rest,
        [flat, part],
        LEFT_SCRATCH,
        operands=(left_one_behind, k_left, far_blocks[1], left_part, turned[1]),
        after=(right_out,),
    )
    left_got = shifted(left_out, "sector", 1)
    position = lax.axis_index("sector")
    first_flag = (position == 0).astype(jnp.int32).reshape(1)
    last_flag = (position == lax.axis_size("sector") - 1).astype(jnp.int32).reshape(1)
    diag = pltpu.VMEM((2, 128, HALF), BF)
    raw = pltpu.VMEM((4, BLK, WB * BLK), BF)
    devices = lax.axis_size("site")
    own, away, second_sum = call(
        second_body,
        [shape((128, 256), F32), shape((128, 256), F32), shape((8, 128), F32)],
        [raw, kept, diag, pltpu.SemaphoreType.DMA],
        smem=1,
        hbm=1,
        operands=(last_flag, right_raw, right_got, left_part, left_far),
        after=(left_out,),
    )
    back = passed_along(away, "site", -1)
    first, sums = call(
        first_body,
        [shape((256, 256), F32), shape((devices, 8, 128), F32)],
        [raw, kept, diag, pltpu.SemaphoreType.DMA],
        smem=1,
        hbm=1,
        operands=(first_flag, left_raw, left_got, right_part, right_far, second_sum),
    )
    gathered = lax.all_to_all(sums, "site", 0, 0, tiled=True)
    return call(
        functools.partial(final_body, 256 * 256 * devices),
        jax.ShapeDtypeStruct((2, 4, BLK, 256), F32),
        operands=(first, own, back, gathered),
    )


def solution(mesh):
    in_specs = (
        P("sector", "site", None, None),
        P("sector", "site", None, None),
        P("sector", "site", None, None),
        P("sector", "site"),
        P("sector", "site", None),
        P(),
        P(),
    )
    out_specs = P("sector", "site", None, None)
    return jax.shard_map(local, mesh=mesh, in_specs=in_specs, out_specs=out_specs, check_vma=False)
```

```python
import functools

import jax
import jax.numpy as jnp
from jax import lax
from jax.experimental import pallas as pl
from jax.experimental.pallas import tpu as pltpu
from jax.sharding import PartitionSpec as P

BLK = 64
PHYS = 4
WB = 17
HALF = WB * 128
FULL = 2 * HALF
GROUPS = 8
DEPTH = 144
BF = jnp.bfloat16
F32 = jnp.float32


def shape(dims, dtype=BF):
    return pltpu.VMEM(dims, dtype)


def call(body, outs, scratch=(), smem=0, hbm=0, operands=(), after=(), mib=16, us=1.20):
    spaces = [pltpu.SMEM] * smem + [pltpu.HBM] * hbm
    spaces += [pltpu.VMEM] * (len(operands) - len(spaces))
    spaces += [pl.ANY] * len(after)
    single = not isinstance(outs, (list, tuple))
    out_specs = [
        pl.BlockSpec(memory_space=pltpu.HBM if getattr(out, "memory_space", None) == pltpu.HBM else pltpu.VMEM)
        for out in ([outs] if single else outs)
    ]
    count = len(operands)
    placed = [
        pltpu.with_memory_space_constraint(value, space) if space == pltpu.HBM else value
        for value, space in zip(operands, spaces)
    ]

    def ordered(*refs):
        body(*refs[:count], *refs[count + len(after) :])

    return pl.pallas_call(
        ordered,
        out_shape=outs,
        in_specs=[pl.BlockSpec(memory_space=space) for space in spaces],
        out_specs=out_specs[0] if single else out_specs,
        scratch_shapes=list(scratch),
        compiler_params=pltpu.CompilerParams(vmem_limit_bytes=mib * 1024 * 1024),
        cost_estimate=pl.CostEstimate(flops=int(us * 1.1e9), bytes_accessed=1, transcendentals=0),
    )(*placed, *after)


def iota(dims, axis):
    return lax.broadcasted_iota(jnp.int32, dims, axis)


def dot(a, b):
    return lax.dot_general(a, b, (((1,), (0,)), ((), ())), preferred_element_type=F32)


def dot_t(a, b):
    return lax.dot_general(a, b, (((1,), (1,)), ((), ())), preferred_element_type=F32)


def target(s, p):
    return (s + p % 2) % 4


def keep_inside(rows_hbm, cols_hbm, mps_hbm, all_ref, high_ref, rows_ref, cols_ref, mps_ref, sems):
    pairs = ((rows_hbm, rows_ref), (cols_hbm, cols_ref), (mps_hbm, mps_ref))
    copies = [pltpu.make_async_copy(a, b, sems.at[i]) for i, (a, b) in enumerate(pairs)]
    for copy in copies:
        copy.start()
    for copy in copies:
        copy.wait()
    row = iota((BLK, 256), 0)
    col = iota((BLK, 256), 1)
    inside = col & (BLK - 1)
    for j in range(2):
        for s in range(4):
            least = jnp.where(col < 64, cols_ref[j, s, 0], cols_ref[j, s, 1])
            most = jnp.where(col < 192, cols_ref[j, s, 2], cols_ref[j, s, 3])
            limit = jnp.where(col < 128, least, most)
            keep = jnp.logical_and(row < rows_ref[j, s], inside < limit)
            kept = jnp.where(keep, mps_ref[j, s].astype(F32), 0.0).astype(BF)
            all_ref[j, s * BLK : (s + 1) * BLK, :] = kept
            high_ref[j, s * BLK : (s + 1) * BLK, :] = kept[:, 128:]


def spread(block, step):
    tiled = jnp.concatenate([block] * 4, axis=1)
    goal = ((iota((256, 256), 0) >> 6) + step) & 3
    return jnp.where(goal == (iota((256, 256), 1) >> 6), tiled, 0.0).astype(BF)


def flipped(values, states):
    turned = values.T
    rows = []
    for t in range(4):
        parts = []
        for p in range(states):
            s = (t - p % 2) % 4
            parts.append(turned[p * BLK : (p + 1) * BLK, s * BLK : (s + 1) * BLK])
        rows.append(jnp.concatenate(parts, axis=1))
    return jnp.concatenate(rows, axis=0).astype(BF)


def enlarge(small, out_ref):
    rows = 4 * WB * 8
    up = jnp.where((iota((rows, 4 * WB), 0) >> 3) == iota((rows, 4 * WB), 1), 1.0, 0.0)
    out = jnp.where((iota((WB, DEPTH), 1) >> 3) == iota((WB, DEPTH), 0), 1.0, 0.0)
    tall = dot(up.astype(BF), small).astype(BF)
    wide = dot(tall, out.astype(BF))
    same = (iota((rows, DEPTH), 0) & 7) == (iota((rows, DEPTH), 1) & 7)
    out_ref[...] = jnp.where(same, wide, 0.0).astype(BF)


def own_ops_body(a_ref, wl_ref, wr_ref, b_ref, at_ref, kl_ref, kr_ref):
    for j in range(2):
        values = a_ref[j].astype(F32)
        for p in range(PHYS):
            b_ref[j, p] = spread(values[:, p * BLK : (p + 1) * BLK], p % 2)
        at_ref[j] = flipped(values[:, :128], 2)
    enlarge(wl_ref[...], kl_ref)
    enlarge(wr_ref[...], kr_ref)


def far_ops_body(a_ref, own_ref, b_ref, at_ref):
    for j in range(2):
        values = a_ref[j].astype(F32)
        for p in range(2):
            b_ref[j, p] = spread(values[:, p * BLK : (p + 1) * BLK], p)
        at_ref[j, :, :128] = own_ref[j]
        at_ref[j, :, 128:] = flipped(values, 2)


def raw_pair(ref, u, lt):
    lane = iota((BLK, 128), 1) < BLK
    if u == WB // 2:
        cols = slice(2 * u * BLK, WB * BLK)
        parts = [ref[2 * lt + i, :, cols].astype(F32) for i in range(2)]
        return jnp.concatenate(parts, axis=1), None
    low = ref[2 * lt, :, u * 128 : (u + 1) * 128].astype(F32)
    high = ref[2 * lt + 1, :, u * 128 : (u + 1) * 128].astype(F32)
    first = jnp.where(lane, low, pltpu.roll(high, BLK, 1))
    second = jnp.where(lane, pltpu.roll(low, BLK, 1), high)
    return first, second


def flat_pair(ref, u, lt):
    at = lt * HALF + 2 * u * 128
    first = ref[:, at : at + 128].astype(F32)
    if u == WB // 2:
        return first, None
    return first, ref[:, at + 128 : at + 256].astype(F32)


def flatten(env_ref, flat_ref):
    for lt in range(2):
        for u in range(9):
            at = lt * HALF + 2 * u * 128
            first, second = raw_pair(env_ref, u, lt)
            flat_ref[:, at : at + 128] = first.astype(BF)
            if second is not None:
                flat_ref[:, at + 128 : at + 256] = second.astype(BF)


def rows_of(flat_ref, e_ref):
    for lt in range(2):
        for w in range(WB):
            at = lt * HALF + w * 128
            e_ref[w * BLK : (w + 1) * BLK, lt * 128 : (lt + 1) * 128] = flat_ref[:, at : at + 128]


def woven(first, second):
    width = first.shape[-1]
    if second is None:
        second = jnp.zeros_like(first)
    parts = [first.reshape(GROUPS, 8, width), second.reshape(GROUPS, 8, width)]
    return jnp.concatenate(parts, axis=1).astype(BF)


def grouped(ref, m_ref):
    for lt in range(2):
        for u in range(9):
            both = woven(*flat_pair(ref, u, lt))
            m_ref[:, u * 16 : (u + 1) * 16, lt * 128 : (lt + 1) * 128] = both


def mixed(m_ref, k, count, h):
    low = dot(k, m_ref[2 * h]).reshape(count * WB, 8, 256)
    high = dot(k, m_ref[2 * h + 1]).reshape(count * WB, 8, 256)
    return jnp.concatenate([low, high], axis=1).astype(BF)


def left_states(e_ref, k_ref, k_at, b_ref, states, m_ref, y_ref, to):
    for p in range(states):
        inner = dot(e_ref[...], b_ref[p])
        for u in range(9):
            first = inner[2 * u * BLK : (2 * u + 1) * BLK]
            second = inner[(2 * u + 1) * BLK : (2 * u + 2) * BLK] if 2 * u + 1 < WB else None
            m_ref[p, :, u * 16 : (u + 1) * 16, :] = woven(first, second)
        k = k_ref[(k_at + p) * WB * 8 : (k_at + p + 1) * WB * 8]
        for h in range(4):
            out = mixed(m_ref.at[p], k, 1, h)
            rows = slice((to + p) * BLK + h * 16, (to + p) * BLK + (h + 1) * 16)
            for v in range(WB):
                for lt in range(2):
                    y_ref[rows, lt * HALF + v * 128 : lt * HALF + (v + 1) * 128] = out[
                        v, :, lt * 128 : (lt + 1) * 128
                    ]


def right_states(m_ref, k, b_ref, b_at, f_ref, y_ref, to):
    for h in range(4):
        f_ref[:, h * 16 : (h + 1) * 16, :] = mixed(m_ref, k, 2, h)
    for p in range(2):
        source = f_ref[p * WB : (p + 1) * WB].reshape(WB * BLK, 256)
        out = dot_t(source, b_ref[b_at + p]).astype(BF)
        rows = slice((to + p) * BLK, (to + p + 1) * BLK)
        for v in range(WB):
            for lt in range(2):
                y_ref[rows, lt * HALF + v * 128 : lt * HALF + (v + 1) * 128] = out[
                    v * BLK : (v + 1) * BLK, lt * 128 : (lt + 1) * 128
                ]


def closed(lhs_ref, own_ref, y_ref, out_ref):
    low = (iota((BLK, HALF), 1) & 127) < BLK
    for lt in range(2):
        cols = slice(lt * HALF, (lt + 1) * HALF)
        inner = jnp.concatenate([own_ref[:, cols], y_ref[:, cols]], axis=0)
        both = dot(lhs_ref[lt * 128 : (lt + 1) * 128, :], inner)
        out_ref[:, cols] = jnp.where(low, both[:BLK], both[BLK:]).astype(BF)


def left_half(flat_ref, k_ref, b_ref, y_ref, e_ref, m_ref):
    rows_of(flat_ref, e_ref)
    left_states(e_ref, k_ref, 0, b_ref, 2, m_ref, y_ref, 0)


def right_half(flat_ref, k_ref, b_ref, y_ref, m_ref, f_ref):
    grouped(flat_ref, m_ref)
    right_states(m_ref, k_ref[: 2 * WB * 8], b_ref, 0, f_ref, y_ref, 0)


def left_far_half(flat_ref, k_ref, b_ref, y_ref, e_ref, m_ref):
    rows_of(flat_ref, e_ref)
    left_states(e_ref, k_ref, 2, b_ref, 2, m_ref, y_ref, 0)


def right_far_half(flat_ref, k_ref, b_ref, y_ref, m_ref, f_ref):
    grouped(flat_ref, m_ref)
    right_states(m_ref, k_ref[2 * WB * 8 :], b_ref, 2, f_ref, y_ref, 0)


def left_rest_raw(env_ref, k_ref, b_ref, own_ref, lhs_ref, out_ref, flat_ref, y_ref, e_ref, m_ref):
    flatten(env_ref, flat_ref)
    left_rest(flat_ref, k_ref, b_ref, own_ref, lhs_ref, out_ref, y_ref, e_ref, m_ref)


def left_rest(flat_ref, k_ref, b_ref, own_ref, lhs_ref, out_ref, y_ref, e_ref, m_ref):
    rows_of(flat_ref, e_ref)
    left_states(e_ref, k_ref, 2, b_ref, 2, m_ref, y_ref, 0)
    closed(lhs_ref, own_ref, y_ref, out_ref)


def right_rest_raw(env_ref, k_ref, b_ref, own_ref, lhs_ref, out_ref, flat_ref, y_ref, m_ref, f_ref):
    flatten(env_ref, flat_ref)
    right_rest(flat_ref, k_ref, b_ref, own_ref, lhs_ref, out_ref, y_ref, m_ref, f_ref)


def right_rest(flat_ref, k_ref, b_ref, own_ref, lhs_ref, out_ref, y_ref, m_ref, f_ref):
    grouped(flat_ref, m_ref)
    right_states(m_ref, k_ref[2 * WB * 8 :], b_ref, 2, f_ref, y_ref, 0)
    closed(lhs_ref, own_ref, y_ref, out_ref)


def prepare(left_hbm, right_hbm, a_ref, wl_ref, wr_ref, b_ref, at_ref, kl_ref, kr_ref, yl_ref, yr_ref, raw_ref, flat_ref, e_ref, m_ref, g_ref, f_ref, sems):
    copies = [
        pltpu.make_async_copy(source, raw_ref.at[i], sems.at[i])
        for i, source in enumerate((left_hbm, right_hbm))
    ]
    for copy in copies:
        copy.start()
    own_ops_body(a_ref, wl_ref, wr_ref, b_ref, at_ref, kl_ref, kr_ref)
    copies[0].wait()
    flatten(raw_ref.at[0], flat_ref.at[0])
    left_half(flat_ref.at[0], kl_ref, b_ref.at[0], yl_ref, e_ref, m_ref)
    copies[1].wait()
    flatten(raw_ref.at[1], flat_ref.at[1])
    right_half(flat_ref.at[1], kr_ref, b_ref.at[1], yr_ref, g_ref, f_ref)


LEFT_SCRATCH = [pltpu.VMEM((WB * BLK, 256), BF), pltpu.VMEM((2, GROUPS, DEPTH, 256), BF)]
RIGHT_SCRATCH = [pltpu.VMEM((GROUPS, DEPTH, 256), BF), pltpu.VMEM((2 * WB, BLK, 256), BF)]


def diagonal(ref, lt, g_ref):
    lane = (iota((BLK, HALF), 1) & 127) < BLK
    low = jnp.where(lane, 1.0, 0.0).astype(BF)
    high = jnp.where(lane, 0.0, 1.0).astype(BF)
    values = ref[:, lt * HALF : (lt + 1) * HALF]
    g_ref[:BLK, :] = values * low
    g_ref[BLK:, :] = values * high


def chosen(flag_ref, edge_hbm, got_ref, raw_ref, flat_ref, g_ref, sem):
    @pl.when(flag_ref[0] == 0)
    def _():
        for lt in range(2):
            diagonal(got_ref, lt, g_ref.at[lt])

    @pl.when(flag_ref[0] != 0)
    def _():
        fetched = pltpu.make_async_copy(edge_hbm, raw_ref, sem)
        fetched.start()
        fetched.wait()
        flatten(raw_ref, flat_ref)
        for lt in range(2):
            diagonal(flat_ref, lt, g_ref.at[lt])


def squared(values):
    return jnp.sum((values * values).reshape(-1, 8, values.shape[1]), axis=0)


def first_body(flag_ref, edge_hbm, got_ref, own_ref, far_ref, sum_ref, out_ref, sums_ref, raw_ref, flat_ref, g_ref, sem):
    chosen(flag_ref, edge_hbm, got_ref, raw_ref, flat_ref, g_ref, sem)
    total = jnp.zeros((8, 256), F32)
    for lt in range(2):
        cols = slice(lt * HALF, (lt + 1) * HALF)
        inner = jnp.concatenate([own_ref[:, cols], far_ref[:, cols]], axis=0)
        out = dot_t(g_ref[lt], inner)
        out_ref[lt * 128 : (lt + 1) * 128, :] = out
        total = total + squared(out)
    second = jnp.sum(sum_ref[...])
    sums_ref[...] = jnp.where(iota(sums_ref.shape, 1) < 4, jnp.sum(total), second)


def second_body(flag_ref, edge_hbm, got_ref, y_ref, far_ref, own_ref, away_ref, sum_ref, raw_ref, flat_ref, g_ref, sem):
    chosen(flag_ref, edge_hbm, got_ref, raw_ref, flat_ref, g_ref, sem)
    total = jnp.zeros((8, 128), F32)
    for lt in range(2):
        cols = slice(lt * HALF, (lt + 1) * HALF)
        inner = jnp.concatenate([y_ref[:, cols], far_ref[:, cols]], axis=0)
        out = dot_t(inner, g_ref[lt])
        own_ref[:, lt * 128 : (lt + 1) * 128] = out[:128]
        away_ref[:, lt * 128 : (lt + 1) * 128] = out[128:]
        total = total + squared(out)
    sum_ref[...] = total


def final_body(entries, first_ref, own_ref, away_ref, sums_ref, out_ref):
    total = jnp.sum(sums_ref[...], axis=0)
    scale = lax.rsqrt(total * (1.0 / entries) + 1e-06)
    for s in range(4):
        out_ref[0, s] = first_ref[s * BLK : (s + 1) * BLK, :] * scale[:1, :1]
        parts = []
        for p in range(PHYS):
            ref, at = (own_ref, p) if p < 2 else (away_ref, p - 2)
            t = target(s, p)
            parts.append(ref[at * BLK : (at + 1) * BLK, t * BLK : (t + 1) * BLK])
        out_ref[1, s] = jnp.concatenate(parts, axis=1) * scale[4:5, :1]


def passed_along(block, axis, distance):
    devices = lax.axis_size(axis)
    route = [(i, (i + distance) % devices) for i in range(devices)]
    return lax.ppermute(block, axis, route)


def shifted(value, axis, by):
    devices = lax.axis_size(axis)
    pairs = [(i, i + by) for i in range(devices) if 0 <= i + by < devices]
    return lax.ppermute(value, axis, pairs)


def local(mps, left_env, right_env, row_fill, col_fill, mpo_values, mpo_pattern):
    left_raw, right_raw = left_env[0], right_env[0]
    left_behind = passed_along(left_raw, "site", 1)
    right_ahead = passed_along(right_raw, "site", -1)
    weights = mpo_values * mpo_pattern.astype(BF)
    left_small = weights.transpose(2, 1, 0).reshape(PHYS * WB, WB)
    right_small = weights.transpose(2, 0, 1).reshape(PHYS * WB, WB)
    masked, high = call(
        keep_inside,
        [shape((2, 256, 256)), shape((2, 256, 128))],
        [
            pltpu.SMEM((2, 4), jnp.int32),
            pltpu.SMEM((2, 4, PHYS), jnp.int32),
            pltpu.VMEM((2, 4, BLK, 256), BF),
            pltpu.SemaphoreType.DMA((3,)),
        ],
        hbm=3,
        operands=(row_fill, col_fill, mps),
    )
    high_behind = passed_along(high, "site", 1)
    rows = 4 * WB * 8
    part, flat = shape((128, FULL)), shape((BLK, FULL))
    blocks, turned_own, k_left, k_right, left_part, right_part = call(
        prepare,
        [
            shape((2, PHYS, 256, 256)),
            shape((2, 256, 128)),
            shape((rows, DEPTH)),
            shape((rows, DEPTH)),
            part,
            part,
        ],
        [
            pltpu.VMEM((2, 4, BLK, WB * BLK), BF),
            pltpu.VMEM((2, BLK, FULL), BF),
            *LEFT_SCRATCH,
            *RIGHT_SCRATCH,
            pltpu.SemaphoreType.DMA((2,)),
        ],
        hbm=2,
        operands=(left_raw, right_raw, masked, left_small, right_small),
        mib=16,
    )
    whole = pltpu.VMEM((128, FULL), BF)
    kept = pltpu.VMEM((BLK, FULL), BF)
    right_one = call(
        right_rest_raw,
        flat,
        [kept, whole, *RIGHT_SCRATCH],
        operands=(right_ahead, k_right, blocks[1], right_part, masked[1]),
        after=(left_part,),
    )
    right_one_ahead = passed_along(right_one, "site", -1)
    far_blocks, turned = call(
        far_ops_body,
        [shape((2, 2, 256, 256)), shape((2, 256, 256))],
        operands=(high_behind, turned_own),
        after=(right_one, left_behind),
        us=0.4,
    )
    left_one = call(
        left_rest_raw,
        flat,
        [kept, whole, *LEFT_SCRATCH],
        operands=(left_behind, k_left, far_blocks[0], left_part, turned[0]),
        after=(right_one,),
    )
    left_one_behind = passed_along(left_one, "site", 1)
    right_part = call(
        right_half, part, RIGHT_SCRATCH, operands=(right_one, k_right, blocks[0]), after=(left_one,)
    )
    left_part = call(left_half, part, LEFT_SCRATCH, operands=(left_one, k_left, blocks[1]))
    right_out = call(
        right_rest,
        flat,
        [whole, *RIGHT_SCRATCH],
        operands=(right_one_ahead, k_right, blocks[0], right_part, masked[0]),
        after=(left_part,),
    )
    right_got = shifted(right_out, "sector", -1)
    right_far = call(
        right_far_half,
        part,
        RIGHT_SCRATCH,
        operands=(right_one_ahead, k_right, blocks[0]),
        after=(right_out,),
        us=0.9,
    )
    left_out = call(
        left_rest,
        flat,
        [whole, *LEFT_SCRATCH],
        operands=(left_one_behind, k_left, far_blocks[1], left_part, turned[1]),
        after=(right_far,),
    )
    left_got = shifted(left_out, "sector", 1)
    left_far = call(
        left_far_half,
        part,
        LEFT_SCRATCH,
        operands=(left_one_behind, k_left, far_blocks[1]),
        after=(left_out,),
        us=1.1,
    )
    position = lax.axis_index("sector")
    first_flag = (position == 0).astype(jnp.int32).reshape(1)
    last_flag = (position == lax.axis_size("sector") - 1).astype(jnp.int32).reshape(1)
    diag = pltpu.VMEM((2, 128, HALF), BF)
    raw = pltpu.VMEM((4, BLK, WB * BLK), BF)
    devices = lax.axis_size("site")
    own, away, second_sum = call(
        second_body,
        [shape((128, 256), F32), shape((128, 256), F32), shape((8, 128), F32)],
        [raw, kept, diag, pltpu.SemaphoreType.DMA],
        smem=1,
        hbm=1,
        operands=(last_flag, right_raw, right_got, left_part, left_far),
        after=(left_out,),
    )
    back = passed_along(away, "site", -1)
    first, sums = call(
        first_body,
        [shape((256, 256), F32), shape((devices, 8, 128), F32)],
        [raw, kept, diag, pltpu.SemaphoreType.DMA],
        smem=1,
        hbm=1,
        operands=(first_flag, left_raw, left_got, right_part, right_far, second_sum),
    )
    gathered = lax.all_to_all(sums, "site", 0, 0, tiled=True)
    return call(
        functools.partial(final_body, 256 * 256 * devices),
        jax.ShapeDtypeStruct((2, 4, BLK, 256), F32),
        operands=(first, own, back, gathered),
    )


def solution(mesh):
    in_specs = (
        P("sector", "site", None, None),
        P("sector", "site", None, None),
        P("sector", "site", None, None),
        P("sector", "site"),
        P("sector", "site", None),
        P(),
        P(),
    )
    out_specs = P("sector", "site", None, None)
    return jax.shard_map(local, mesh=mesh, in_specs=in_specs, out_specs=out_specs, check_vma=False)
```

```python
import functools

import jax
import jax.numpy as jnp
from jax import lax
from jax.experimental import pallas as pl
from jax.experimental.pallas import tpu as pltpu
from jax.sharding import PartitionSpec as P

BLK = 64
PHYS = 4
WB = 17
HALF = WB * 128
FULL = 2 * HALF
GROUPS = 8
DEPTH = 144
BF = jnp.bfloat16
F32 = jnp.float32


def shape(dims, dtype=BF):
    return pltpu.VMEM(dims, dtype)


def call(body, outs, scratch=(), smem=0, hbm=0, operands=(), after=(), mib=16, us=1.20):
    spaces = [pltpu.SMEM] * smem + [pltpu.HBM] * hbm
    spaces += [pltpu.VMEM] * (len(operands) - len(spaces))
    spaces += [pl.ANY] * len(after)
    single = not isinstance(outs, (list, tuple))
    out_specs = [
        pl.BlockSpec(memory_space=pltpu.HBM if getattr(out, "memory_space", None) == pltpu.HBM else pltpu.VMEM)
        for out in ([outs] if single else outs)
    ]
    count = len(operands)
    placed = [
        pltpu.with_memory_space_constraint(value, space) if space == pltpu.HBM else value
        for value, space in zip(operands, spaces)
    ]

    def ordered(*refs):
        body(*refs[:count], *refs[count + len(after) :])

    return pl.pallas_call(
        ordered,
        out_shape=outs,
        in_specs=[pl.BlockSpec(memory_space=space) for space in spaces],
        out_specs=out_specs[0] if single else out_specs,
        scratch_shapes=list(scratch),
        compiler_params=pltpu.CompilerParams(vmem_limit_bytes=mib * 1024 * 1024),
        cost_estimate=pl.CostEstimate(flops=int(us * 1.1e9), bytes_accessed=1, transcendentals=0),
    )(*placed, *after)


def iota(dims, axis):
    return lax.broadcasted_iota(jnp.int32, dims, axis)


def dot(a, b):
    return lax.dot_general(a, b, (((1,), (0,)), ((), ())), preferred_element_type=F32)


def dot_t(a, b):
    return lax.dot_general(a, b, (((1,), (1,)), ((), ())), preferred_element_type=F32)


def target(s, p):
    return (s + p % 2) % 4


def keep_inside(rows_hbm, cols_hbm, mps_hbm, all_ref, high_ref, rows_ref, cols_ref, mps_ref, sems):
    pairs = ((rows_hbm, rows_ref), (cols_hbm, cols_ref), (mps_hbm, mps_ref))
    copies = [pltpu.make_async_copy(a, b, sems.at[i]) for i, (a, b) in enumerate(pairs)]
    for copy in copies:
        copy.start()
    for copy in copies:
        copy.wait()
    row = iota((BLK, 256), 0)
    col = iota((BLK, 256), 1)
    inside = col & (BLK - 1)
    for j in range(2):
        for s in range(4):
            least = jnp.where(col < 64, cols_ref[j, s, 0], cols_ref[j, s, 1])
            most = jnp.where(col < 192, cols_ref[j, s, 2], cols_ref[j, s, 3])
            limit = jnp.where(col < 128, least, most)
            keep = jnp.logical_and(row < rows_ref[j, s], inside < limit)
            kept = jnp.where(keep, mps_ref[j, s].astype(F32), 0.0).astype(BF)
            all_ref[j, s * BLK : (s + 1) * BLK, :] = kept
            high_ref[j, s * BLK : (s + 1) * BLK, :] = kept[:, 128:]


def spread(block, step):
    tiled = jnp.concatenate([block] * 4, axis=1)
    goal = ((iota((256, 256), 0) >> 6) + step) & 3
    return jnp.where(goal == (iota((256, 256), 1) >> 6), tiled, 0.0).astype(BF)


def flipped(values, states):
    turned = values.T
    rows = []
    for t in range(4):
        parts = []
        for p in range(states):
            s = (t - p % 2) % 4
            parts.append(turned[p * BLK : (p + 1) * BLK, s * BLK : (s + 1) * BLK])
        rows.append(jnp.concatenate(parts, axis=1))
    return jnp.concatenate(rows, axis=0).astype(BF)


def enlarge(small, out_ref):
    rows = 4 * WB * 8
    up = jnp.where((iota((rows, 4 * WB), 0) >> 3) == iota((rows, 4 * WB), 1), 1.0, 0.0)
    out = jnp.where((iota((WB, DEPTH), 1) >> 3) == iota((WB, DEPTH), 0), 1.0, 0.0)
    tall = dot(up.astype(BF), small).astype(BF)
    wide = dot(tall, out.astype(BF))
    same = (iota((rows, DEPTH), 0) & 7) == (iota((rows, DEPTH), 1) & 7)
    out_ref[...] = jnp.where(same, wide, 0.0).astype(BF)


def own_ops_body(a_ref, wl_ref, wr_ref, b_ref, at_ref, kl_ref, kr_ref):
    for j in range(2):
        values = a_ref[j].astype(F32)
        for p in range(PHYS):
            b_ref[j, p] = spread(values[:, p * BLK : (p + 1) * BLK], p % 2)
        at_ref[j] = flipped(values[:, :128], 2)
    enlarge(wl_ref[...], kl_ref)
    enlarge(wr_ref[...], kr_ref)


def far_ops_body(j, a_ref, own_ref, b_ref, at_ref):
    values = a_ref[j].astype(F32)
    for p in range(2):
        b_ref[p] = spread(values[:, p * BLK : (p + 1) * BLK], p)
    at_ref[:, :128] = own_ref[j]
    at_ref[:, 128:] = flipped(values, 2)


def raw_pair(ref, u, lt):
    lane = iota((BLK, 128), 1) < BLK
    if u == WB // 2:
        cols = slice(2 * u * BLK, WB * BLK)
        parts = [ref[2 * lt + i, :, cols].astype(F32) for i in range(2)]
        return jnp.concatenate(parts, axis=1), None
    low = ref[2 * lt, :, u * 128 : (u + 1) * 128].astype(F32)
    high = ref[2 * lt + 1, :, u * 128 : (u + 1) * 128].astype(F32)
    first = jnp.where(lane, low, pltpu.roll(high, BLK, 1))
    second = jnp.where(lane, pltpu.roll(low, BLK, 1), high)
    return first, second


def flat_pair(ref, u, lt):
    at = lt * HALF + 2 * u * 128
    first = ref[:, at : at + 128].astype(F32)
    if u == WB // 2:
        return first, None
    return first, ref[:, at + 128 : at + 256].astype(F32)


def flatten(env_ref, flat_ref):
    for lt in range(2):
        for u in range(9):
            at = lt * HALF + 2 * u * 128
            first, second = raw_pair(env_ref, u, lt)
            flat_ref[:, at : at + 128] = first.astype(BF)
            if second is not None:
                flat_ref[:, at + 128 : at + 256] = second.astype(BF)


def rows_of(flat_ref, e_ref):
    for lt in range(2):
        for w in range(WB):
            at = lt * HALF + w * 128
            e_ref[w * BLK : (w + 1) * BLK, lt * 128 : (lt + 1) * 128] = flat_ref[:, at : at + 128]


def woven(first, second):
    width = first.shape[-1]
    if second is None:
        second = jnp.zeros_like(first)
    parts = [first.reshape(GROUPS, 8, width), second.reshape(GROUPS, 8, width)]
    return jnp.concatenate(parts, axis=1).astype(BF)


def grouped(ref, m_ref):
    for lt in range(2):
        for u in range(9):
            both = woven(*flat_pair(ref, u, lt))
            m_ref[:, u * 16 : (u + 1) * 16, lt * 128 : (lt + 1) * 128] = both


def mixed(m_ref, k, count, h):
    low = dot(k, m_ref[2 * h]).reshape(count * WB, 8, 256)
    high = dot(k, m_ref[2 * h + 1]).reshape(count * WB, 8, 256)
    return jnp.concatenate([low, high], axis=1).astype(BF)


def left_states(e_ref, k_ref, k_at, b_ref, states, m_ref, y_ref, to):
    for p in range(states):
        inner = dot(e_ref[...], b_ref[p])
        for u in range(9):
            first = inner[2 * u * BLK : (2 * u + 1) * BLK]
            second = inner[(2 * u + 1) * BLK : (2 * u + 2) * BLK] if 2 * u + 1 < WB else None
            m_ref[p, :, u * 16 : (u + 1) * 16, :] = woven(first, second)
        k = k_ref[(k_at + p) * WB * 8 : (k_at + p + 1) * WB * 8]
        for h in range(4):
            out = mixed(m_ref.at[p], k, 1, h)
            rows = slice((to + p) * BLK + h * 16, (to + p) * BLK + (h + 1) * 16)
            for v in range(WB):
                for lt in range(2):
                    y_ref[rows, lt * HALF + v * 128 : lt * HALF + (v + 1) * 128] = out[
                        v, :, lt * 128 : (lt + 1) * 128
                    ]


def right_states(m_ref, k, b_ref, b_at, f_ref, y_ref, to):
    for h in range(4):
        f_ref[:, h * 16 : (h + 1) * 16, :] = mixed(m_ref, k, 2, h)
    for p in range(2):
        source = f_ref[p * WB : (p + 1) * WB].reshape(WB * BLK, 256)
        out = dot_t(source, b_ref[b_at + p]).astype(BF)
        rows = slice((to + p) * BLK, (to + p + 1) * BLK)
        for v in range(WB):
            for lt in range(2):
                y_ref[rows, lt * HALF + v * 128 : lt * HALF + (v + 1) * 128] = out[
                    v * BLK : (v + 1) * BLK, lt * 128 : (lt + 1) * 128
                ]


def closed(lhs_ref, own_ref, y_ref, out_ref):
    low = (iota((BLK, HALF), 1) & 127) < BLK
    for lt in range(2):
        cols = slice(lt * HALF, (lt + 1) * HALF)
        inner = jnp.concatenate([own_ref[:, cols], y_ref[:, cols]], axis=0)
        both = dot(lhs_ref[lt * 128 : (lt + 1) * 128, :], inner)
        out_ref[:, cols] = jnp.where(low, both[:BLK], both[BLK:]).astype(BF)


def left_half(flat_ref, k_ref, b_ref, y_ref, e_ref, m_ref):
    rows_of(flat_ref, e_ref)
    left_states(e_ref, k_ref, 0, b_ref, 2, m_ref, y_ref, 0)


def right_half(flat_ref, k_ref, b_ref, y_ref, m_ref, f_ref):
    grouped(flat_ref, m_ref)
    right_states(m_ref, k_ref[: 2 * WB * 8], b_ref, 0, f_ref, y_ref, 0)


def left_far_half(flat_ref, k_ref, b_ref, y_ref, e_ref, m_ref):
    rows_of(flat_ref, e_ref)
    left_states(e_ref, k_ref, 2, b_ref, 2, m_ref, y_ref, 0)


def right_far_half(flat_ref, k_ref, b_ref, y_ref, m_ref, f_ref):
    grouped(flat_ref, m_ref)
    right_states(m_ref, k_ref[2 * WB * 8 :], b_ref, 2, f_ref, y_ref, 0)


def left_rest_raw(env_ref, k_ref, b_ref, own_ref, lhs_ref, out_ref, flat_ref, y_ref, e_ref, m_ref):
    flatten(env_ref, flat_ref)
    left_rest(flat_ref, k_ref, b_ref, own_ref, lhs_ref, out_ref, y_ref, e_ref, m_ref)


def left_rest(flat_ref, k_ref, b_ref, own_ref, lhs_ref, out_ref, y_ref, e_ref, m_ref):
    rows_of(flat_ref, e_ref)
    left_states(e_ref, k_ref, 2, b_ref, 2, m_ref, y_ref, 0)
    closed(lhs_ref, own_ref, y_ref, out_ref)


def right_rest_raw(env_ref, k_ref, b_ref, own_ref, lhs_ref, out_ref, flat_ref, y_ref, m_ref, f_ref):
    flatten(env_ref, flat_ref)
    right_rest(flat_ref, k_ref, b_ref, own_ref, lhs_ref, out_ref, y_ref, m_ref, f_ref)


def right_rest(flat_ref, k_ref, b_ref, own_ref, lhs_ref, out_ref, y_ref, m_ref, f_ref):
    grouped(flat_ref, m_ref)
    right_states(m_ref, k_ref[2 * WB * 8 :], b_ref, 2, f_ref, y_ref, 0)
    closed(lhs_ref, own_ref, y_ref, out_ref)


def prepare(left_hbm, right_hbm, a_ref, wl_ref, wr_ref, b_ref, at_ref, kl_ref, kr_ref, yl_ref, yr_ref, raw_ref, flat_ref, e_ref, m_ref, g_ref, f_ref, sems):
    copies = [
        pltpu.make_async_copy(source, raw_ref.at[i], sems.at[i])
        for i, source in enumerate((left_hbm, right_hbm))
    ]
    for copy in copies:
        copy.start()
    own_ops_body(a_ref, wl_ref, wr_ref, b_ref, at_ref, kl_ref, kr_ref)
    copies[0].wait()
    flatten(raw_ref.at[0], flat_ref.at[0])
    left_half(flat_ref.at[0], kl_ref, b_ref.at[0], yl_ref, e_ref, m_ref)
    copies[1].wait()
    flatten(raw_ref.at[1], flat_ref.at[1])
    right_half(flat_ref.at[1], kr_ref, b_ref.at[1], yr_ref, g_ref, f_ref)


LEFT_SCRATCH = [pltpu.VMEM((WB * BLK, 256), BF), pltpu.VMEM((2, GROUPS, DEPTH, 256), BF)]
RIGHT_SCRATCH = [pltpu.VMEM((GROUPS, DEPTH, 256), BF), pltpu.VMEM((2 * WB, BLK, 256), BF)]


def diagonal(ref, lt, g_ref):
    lane = (iota((BLK, HALF), 1) & 127) < BLK
    low = jnp.where(lane, 1.0, 0.0).astype(BF)
    high = jnp.where(lane, 0.0, 1.0).astype(BF)
    values = ref[:, lt * HALF : (lt + 1) * HALF]
    g_ref[:BLK, :] = values * low
    g_ref[BLK:, :] = values * high


def chosen(flag_ref, edge_hbm, got_ref, raw_ref, flat_ref, g_ref, sem):
    @pl.when(flag_ref[0] == 0)
    def _():
        for lt in range(2):
            diagonal(got_ref, lt, g_ref.at[lt])

    @pl.when(flag_ref[0] != 0)
    def _():
        fetched = pltpu.make_async_copy(edge_hbm, raw_ref, sem)
        fetched.start()
        fetched.wait()
        flatten(raw_ref, flat_ref)
        for lt in range(2):
            diagonal(flat_ref, lt, g_ref.at[lt])


def squared(values):
    return jnp.sum((values * values).reshape(-1, 8, values.shape[1]), axis=0)


def first_body(flag_ref, edge_hbm, got_ref, own_ref, far_ref, sum_ref, out_ref, sums_ref, raw_ref, flat_ref, g_ref, sem):
    chosen(flag_ref, edge_hbm, got_ref, raw_ref, flat_ref, g_ref, sem)
    total = jnp.zeros((8, 256), F32)
    for lt in range(2):
        cols = slice(lt * HALF, (lt + 1) * HALF)
        inner = jnp.concatenate([own_ref[:, cols], far_ref[:, cols]], axis=0)
        out = dot_t(g_ref[lt], inner)
        out_ref[lt * 128 : (lt + 1) * 128, :] = out
        total = total + squared(out)
    second = jnp.sum(sum_ref[...])
    sums_ref[...] = jnp.where(iota(sums_ref.shape, 1) < 4, jnp.sum(total), second)


def second_body(flag_ref, edge_hbm, got_ref, y_ref, far_ref, own_ref, away_ref, sum_ref, raw_ref, flat_ref, g_ref, sem):
    chosen(flag_ref, edge_hbm, got_ref, raw_ref, flat_ref, g_ref, sem)
    total = jnp.zeros((8, 128), F32)
    for lt in range(2):
        cols = slice(lt * HALF, (lt + 1) * HALF)
        inner = jnp.concatenate([y_ref[:, cols], far_ref[:, cols]], axis=0)
        out = dot_t(inner, g_ref[lt])
        own_ref[:, lt * 128 : (lt + 1) * 128] = out[:128]
        away_ref[:, lt * 128 : (lt + 1) * 128] = out[128:]
        total = total + squared(out)
    sum_ref[...] = total


def final_body(entries, first_ref, own_ref, away_ref, sums_ref, out_ref):
    total = jnp.sum(sums_ref[...], axis=0)
    scale = lax.rsqrt(total * (1.0 / entries) + 1e-06)
    for s in range(4):
        out_ref[0, s] = first_ref[s * BLK : (s + 1) * BLK, :] * scale[:1, :1]
        parts = []
        for p in range(PHYS):
            ref, at = (own_ref, p) if p < 2 else (away_ref, p - 2)
            t = target(s, p)
            parts.append(ref[at * BLK : (at + 1) * BLK, t * BLK : (t + 1) * BLK])
        out_ref[1, s] = jnp.concatenate(parts, axis=1) * scale[4:5, :1]


def passed_along(block, axis, distance):
    devices = lax.axis_size(axis)
    route = [(i, (i + distance) % devices) for i in range(devices)]
    return lax.ppermute(block, axis, route)


def shifted(value, axis, by):
    devices = lax.axis_size(axis)
    pairs = [(i, i + by) for i in range(devices) if 0 <= i + by < devices]
    return lax.ppermute(value, axis, pairs)


def local(mps, left_env, right_env, row_fill, col_fill, mpo_values, mpo_pattern):
    left_raw, right_raw = left_env[0], right_env[0]
    left_behind = passed_along(left_raw, "site", 1)
    right_ahead = passed_along(right_raw, "site", -1)
    weights = mpo_values * mpo_pattern.astype(BF)
    left_small = weights.transpose(2, 1, 0).reshape(PHYS * WB, WB)
    right_small = weights.transpose(2, 0, 1).reshape(PHYS * WB, WB)
    masked, high = call(
        keep_inside,
        [shape((2, 256, 256)), shape((2, 256, 128))],
        [
            pltpu.SMEM((2, 4), jnp.int32),
            pltpu.SMEM((2, 4, PHYS), jnp.int32),
            pltpu.VMEM((2, 4, BLK, 256), BF),
            pltpu.SemaphoreType.DMA((3,)),
        ],
        hbm=3,
        operands=(row_fill, col_fill, mps),
    )
    high_behind = passed_along(high, "site", 1)
    rows = 4 * WB * 8
    part, flat = shape((128, FULL)), shape((BLK, FULL))
    blocks, turned_own, k_left, k_right, left_part, right_part = call(
        prepare,
        [
            shape((2, PHYS, 256, 256)),
            shape((2, 256, 128)),
            shape((rows, DEPTH)),
            shape((rows, DEPTH)),
            part,
            part,
        ],
        [
            pltpu.VMEM((2, 4, BLK, WB * BLK), BF),
            pltpu.VMEM((2, BLK, FULL), BF),
            *LEFT_SCRATCH,
            *RIGHT_SCRATCH,
            pltpu.SemaphoreType.DMA((2,)),
        ],
        hbm=2,
        operands=(left_raw, right_raw, masked, left_small, right_small),
        mib=16,
    )
    whole = pltpu.VMEM((128, FULL), BF)
    kept = pltpu.VMEM((BLK, FULL), BF)
    right_one = call(
        right_rest_raw,
        flat,
        [kept, whole, *RIGHT_SCRATCH],
        operands=(right_ahead, k_right, blocks[1], right_part, masked[1]),
        after=(left_part,),
    )
    right_one_ahead = passed_along(right_one, "site", -1)
    far_outs = [shape((2, 256, 256)), shape((256, 256))]
    first_far, first_turned = call(
        functools.partial(far_ops_body, 0),
        far_outs,
        operands=(high_behind, turned_own),
        after=(right_one, left_behind),
        us=0.4,
    )
    left_one = call(
        left_rest_raw,
        flat,
        [kept, whole, *LEFT_SCRATCH],
        operands=(left_behind, k_left, first_far, left_part, first_turned),
        after=(right_one,),
    )
    left_one_behind = passed_along(left_one, "site", 1)
    second_far, second_turned = call(
        functools.partial(far_ops_body, 1),
        far_outs,
        operands=(high_behind, turned_own),
        after=(left_one,),
        us=0.4,
    )
    right_part = call(
        right_half, part, RIGHT_SCRATCH, operands=(right_one, k_right, blocks[0]), after=(left_one,)
    )
    left_part = call(left_half, part, LEFT_SCRATCH, operands=(left_one, k_left, blocks[1]))
    right_out = call(
        right_rest,
        flat,
        [whole, *RIGHT_SCRATCH],
        operands=(right_one_ahead, k_right, blocks[0], right_part, masked[0]),
        after=(left_part,),
    )
    right_got = shifted(right_out, "sector", -1)
    right_far = call(
        right_far_half,
        part,
        RIGHT_SCRATCH,
        operands=(right_one_ahead, k_right, blocks[0]),
        after=(right_out,),
        us=0.9,
    )
    left_out = call(
        left_rest,
        flat,
        [whole, *LEFT_SCRATCH],
        operands=(left_one_behind, k_left, second_far, left_part, second_turned),
        after=(right_far,),
    )
    left_got = shifted(left_out, "sector", 1)
    left_far = call(
        left_far_half,
        part,
        LEFT_SCRATCH,
        operands=(left_one_behind, k_left, second_far),
        after=(left_out,),
        us=1.1,
    )
    position = lax.axis_index("sector")
    first_flag = (position == 0).astype(jnp.int32).reshape(1)
    last_flag = (position == lax.axis_size("sector") - 1).astype(jnp.int32).reshape(1)
    diag = pltpu.VMEM((2, 128, HALF), BF)
    raw = pltpu.VMEM((4, BLK, WB * BLK), BF)
    devices = lax.axis_size("site")
    own, away, second_sum = call(
        second_body,
        [shape((128, 256), F32), shape((128, 256), F32), shape((8, 128), F32)],
        [raw, kept, diag, pltpu.SemaphoreType.DMA],
        smem=1,
        hbm=1,
        operands=(last_flag, right_raw, right_got, left_part, left_far),
        after=(left_out,),
    )
    back = passed_along(away, "site", -1)
    first, sums = call(
        first_body,
        [shape((256, 256), F32), shape((devices, 8, 128), F32)],
        [raw, kept, diag, pltpu.SemaphoreType.DMA],
        smem=1,
        hbm=1,
        operands=(first_flag, left_raw, left_got, right_part, right_far, second_sum),
    )
    gathered = lax.all_to_all(sums, "site", 0, 0, tiled=True)
    return call(
        functools.partial(final_body, 256 * 256 * devices),
        jax.ShapeDtypeStruct((2, 4, BLK, 256), F32),
        operands=(first, own, back, gathered),
    )


def solution(mesh):
    in_specs = (
        P("sector", "site", None, None),
        P("sector", "site", None, None),
        P("sector", "site", None, None),
        P("sector", "site"),
        P("sector", "site", None),
        P(),
        P(),
    )
    out_specs = P("sector", "site", None, None)
    return jax.shard_map(local, mesh=mesh, in_specs=in_specs, out_specs=out_specs, check_vma=False)
```
